32 devices in a mesh: mem: 8 (over z, y), reg: 4 (over x, core).
Axes of the slice: x: 2, y: 2, z: 4, core: 2. Of those that a mesh axis runs over, the one named last changes fastest.
Arguments:
- prior_members_field: bfloat16 [1024, 4, 8, 2048], P('mem', 'reg'), may hold values from -6 to 6
- measure_space_deviations: bfloat16 [1024, 4, 8, 1024], P('mem', 'reg'), may hold values from -12 to 12
- measured_minus_predicted: bfloat16 [4, 8, 1024], P('reg'), may hold values from -12 to 12
- measure_pool_indices: int32 [4, 8, 1024], P('reg'), may hold values from 0 to 5119
- active_measure_tally: int32 [4, 8], P('reg', 'mem'), may hold values from 256 to 1024, as said below
- tapered_error_weight: float32 [4, 8, 1024], P('reg', 'mem'), may hold values from 0.02 to 0.5
Outputs:
- analysis: bfloat16 [1024, 4, 8, 2048], P('mem', 'reg')
The draws below stay inside these ranges and needn't reach their ends.
Inputs may be any that keep to these rules, and one draw needn't show every extreme that they name: `active_measure_tally`: some block has exactly 1024 live entries.
All inputs are finite; a program needn't handle non-finite values.
Results may differ from the reference program's by a relative error of at most 0.0089.
Values may be sent and summed in bfloat16 or wider, within the bound.
No kernel may reach another device: no remote copies, remote signals or barrier semaphores. Data moves between devices by JAX's collectives and lax.ppermute only.
A program may use at most 128 MiB of HBM per device.

```python
import math
import jax
import jax.numpy as jnp
from jax import lax

MEMBER_TOTAL = 1024
OBS_BLK = 1024
OBS_USE = 1024
ITERS = 2
TILE_ENTRIES = 2048
STRIP_TOTAL = 4
TILES_PER_STRIP = 8


def draw_active_measure_tally(key, part):
    key = jax.random.fold_in(key, 7)
    key_counts, key_spot = jax.random.split(key)
    counts = jax.random.randint(key_counts, (STRIP_TOTAL * TILES_PER_STRIP,), OBS_USE // 4, OBS_USE + 1)
    chosen_spot = jax.random.randint(key_spot, (), 0, STRIP_TOTAL * TILES_PER_STRIP)
    flat_counts = jnp.where(jnp.arange(STRIP_TOTAL * TILES_PER_STRIP) == chosen_spot, OBS_USE, counts)
    return flat_counts.reshape(STRIP_TOTAL, TILES_PER_STRIP).astype(jnp.int32)


def set_ends(result, rng, smallest, largest):
    longest = result.shape.index(max(result.shape))
    spots = []
    for shift in (0, 1):
        where = [jax.random.randint(jax.random.fold_in(rng, axis), (), 0, length) for axis, length in enumerate(result.shape)]
        where[longest] = (where[longest] + shift) % result.shape[longest]
        spots.append(tuple(where))
    return result.at[spots[0]].set(smallest).at[spots[1]].set(largest)


def steps_of(rng, dims, shards, smallest, high):
    loudness, own = 1.0, jax.random.fold_in(rng, 6)
    for dim, blocks in shards:
        steps = jnp.exp(jax.random.uniform(jax.random.fold_in(own, dim), (blocks,), jnp.float32, smallest / len(shards), high / len(shards)))
        loudness = loudness * jnp.repeat(steps, dims[dim] // blocks).reshape([-1 if axis == dim else 1 for axis in range(len(dims))])
    return loudness


def scatter_about(key, dims, scale, limit, cuts=(), kind=jnp.bfloat16):
    drawn = scale * jax.random.normal(key, dims, jnp.float32)
    if cuts:
        drawn = drawn * steps_of(key, dims, cuts, -0.22, 0.18)
    return jnp.clip(drawn, -limit, limit).astype(kind)


def setup_inputs(seed: int = 0) -> dict:
    splits = jax.random.split(jax.random.key(seed), 7)
    prior_members_field = scatter_about(splits[0], (MEMBER_TOTAL, STRIP_TOTAL, TILES_PER_STRIP, TILE_ENTRIES), 1.0, 6.0, ((0, 8), (1, 4)))
    measure_space_deviations = scatter_about(splits[1], (MEMBER_TOTAL, STRIP_TOTAL, TILES_PER_STRIP, OBS_BLK), 2.0, 12.0, ((0, 8), (1, 4)))
    measured_minus_predicted = scatter_about(splits[2], (STRIP_TOTAL, TILES_PER_STRIP, OBS_BLK), 2.0, 12.0, ((0, 4),))
    measure_pool_indices = set_ends(jax.random.randint(splits[3], (STRIP_TOTAL, TILES_PER_STRIP, OBS_USE), 0, 5 * OBS_BLK), jax.random.fold_in(splits[3], 1), 0, (5 * OBS_BLK) - 1).astype(jnp.int32)
    active_measure_tally = draw_active_measure_tally(jax.random.fold_in(splits[6], 71), 0)
    tapered_error_weight = jnp.clip(jnp.exp(math.log(0.5) - 3.218876 * jax.random.uniform(splits[5], (STRIP_TOTAL, TILES_PER_STRIP, OBS_USE), jnp.float32) ** steps_of(splits[5], (STRIP_TOTAL, TILES_PER_STRIP, OBS_USE), ((0, 4), (1, 8)), -0.2, 0.2)), 0.02, 0.5)
    return {"prior_members_field": prior_members_field, "measure_space_deviations": measure_space_deviations, "measured_minus_predicted": measured_minus_predicted, "measure_pool_indices": measure_pool_indices, "active_measure_tally": active_measure_tally, "tapered_error_weight": tapered_error_weight}


def ensemble_transform(obs_rows, innov_row, obs_weight):
    count_k = obs_rows.shape[0]
    identity = jnp.eye(count_k, dtype=jnp.float32)
    weighted = (obs_rows.astype(jnp.float32) * obs_weight[None, :]).astype(jnp.bfloat16)
    precision_mat = lax.dot_general(weighted, obs_rows, (((1,), (1,)), ((), ())), preferred_element_type=jnp.float32)
    precision_mat = precision_mat + (count_k - 1.0) * identity
    trace_mean = jnp.trace(precision_mat) / count_k
    root_iter = (precision_mat / trace_mean).astype(jnp.bfloat16)
    inverse_iter = identity.astype(jnp.bfloat16)
    for repeat in range(ITERS):
        product = jnp.dot(inverse_iter, root_iter, preferred_element_type=jnp.float32)
        newton_step = (1.5 * identity - 0.5 * product).astype(jnp.bfloat16)
        if repeat + 1 < ITERS:
            root_iter = jnp.dot(root_iter, newton_step, preferred_element_type=jnp.float32).astype(jnp.bfloat16)
        inverse_iter = jnp.dot(newton_step, inverse_iter, preferred_element_type=jnp.float32).astype(jnp.bfloat16)
    gain_vector = jnp.dot(weighted, innov_row, preferred_element_type=jnp.float32)
    inv_root = inverse_iter.astype(jnp.float32)
    inner = jnp.dot(inv_root, gain_vector, precision=lax.Precision.HIGHEST)
    mean_weight = jnp.dot(inv_root, inner, precision=lax.Precision.HIGHEST) / trace_mean
    spread_factor = jnp.sqrt((count_k - 1.0) / trace_mean)
    return (spread_factor * inv_root + mean_weight[:, None]).astype(jnp.bfloat16)

def apply_transform(transform, tile_model_entries):
    state_mean = lax.optimization_barrier(jnp.mean(tile_model_entries.astype(jnp.float32), axis=0))
    perturb = (tile_model_entries.astype(jnp.float32) - state_mean[None, :]).astype(jnp.bfloat16)
    increment = lax.dot_general(transform, perturb, (((0,), (0,)), ((), ())), preferred_element_type=jnp.float32)
    return (state_mean[None, :] + increment).astype(jnp.bfloat16)

def reference(prior_members_field, measure_space_deviations, measured_minus_predicted, measure_pool_indices, active_measure_tally, tapered_error_weight):
    obs_pool = jnp.concatenate([measure_space_deviations, measured_minus_predicted[None]], axis=0)
    padded = jnp.pad(obs_pool, ((0, 0), (1, 1), (1, 1), (0, 0)))
    rows_total = obs_pool.shape[0]
    slots = jnp.arange(OBS_USE, dtype=jnp.int32)

    def one_block(block_index):
        strip_coordinate = (block_index // TILES_PER_STRIP).astype(jnp.int32)
        meridian_coordinate = (block_index % TILES_PER_STRIP).astype(jnp.int32)
        nought_constant = jnp.zeros((), jnp.int32)
        window = lax.dynamic_slice(padded, (nought_constant, strip_coordinate, meridian_coordinate, nought_constant), (rows_total, 3, 3, OBS_BLK))
        neighbours = jnp.concatenate([window[:, 1, 1], window[:, 0, 1], window[:, 2, 1], window[:, 1, 0], window[:, 1, 2]], axis=1)
        chosen = jnp.take(neighbours, measure_pool_indices[strip_coordinate, meridian_coordinate], axis=1)
        obs_weight = jnp.where(slots < active_measure_tally[strip_coordinate, meridian_coordinate], tapered_error_weight[strip_coordinate, meridian_coordinate], 0.0).astype(jnp.float32)
        transform = ensemble_transform(chosen[:-1], chosen[-1], obs_weight)
        tile_model_entries = lax.dynamic_slice(prior_members_field, (nought_constant, strip_coordinate, meridian_coordinate, nought_constant), (MEMBER_TOTAL, 1, 1, TILE_ENTRIES))[:, 0, 0]
        return apply_transform(transform, tile_model_entries)
    blocks = lax.map(one_block, jnp.arange(STRIP_TOTAL * TILES_PER_STRIP, dtype=jnp.int32))
    return jnp.transpose(blocks.reshape(STRIP_TOTAL, TILES_PER_STRIP, MEMBER_TOTAL, TILE_ENTRIES), (2, 0, 1, 3))
```

```python
import functools

import jax
import jax.numpy as jnp
from jax import lax
from jax.experimental import pallas as pl
from jax.experimental.pallas import tpu as pltpu
from jax.sharding import PartitionSpec as P

ITERS = 2
INNOV_ROWS = 16
SLOT_CHUNK = 256
MIB = 1024 * 1024


def gather_kernel(own_ref, up_ref, down_ref, inn_own, inn_up, inn_down, idx_ref, out_ref, inn_ref):
    block = pl.program_id(0)
    blocks = own_ref.shape[0]
    depth = own_ref.shape[2]
    members = own_ref.shape[1]
    west = jnp.maximum(block - 1, 0)
    east = jnp.minimum(block + 1, blocks - 1)
    slots = out_ref.shape[2]
    sources = (
        (own_ref, inn_own, block, None),
        (up_ref, inn_up, block, None),
        (down_ref, inn_down, block, None),
        (own_ref, inn_own, west, block > 0),
        (own_ref, inn_own, east, block < blocks - 1),
    )
    rows = lax.broadcasted_iota(jnp.int32, (depth, SLOT_CHUNK), 0)

    @pl.loop(0, slots // SLOT_CHUNK)
    def _(chunk):
        where = pl.ds(pl.multiple_of(chunk * SLOT_CHUNK, SLOT_CHUNK), SLOT_CHUNK)
        picks = idx_ref[pl.ds(block, 1), where]
        acc = jnp.zeros((members + INNOV_ROWS, SLOT_CHUNK), jnp.float32)
        for number, (ref, inn, at, live) in enumerate(sources):
            local = picks - number * depth
            if live is not None:
                local = jnp.where(live, local, -1)
            one_hot = jnp.where(rows == local, 1.0, 0.0).astype(jnp.bfloat16)
            lhs = jnp.concatenate([ref[at], inn[at]], axis=0)
            acc += jnp.dot(lhs, one_hot, preferred_element_type=jnp.float32)
        out_ref[0, :, where] = acc[:members].astype(jnp.bfloat16)
        inn_ref[0, :, where] = acc[members:].astype(jnp.bfloat16)


def gather_chosen(own, up, down, inn_own, inn_up, inn_down, picks):
    blocks, members, depth = own.shape
    slots = picks.shape[1]
    vmem = pl.BlockSpec(memory_space=pltpu.VMEM)
    return pl.pallas_call(
        gather_kernel,
        grid=(blocks,),
        in_specs=[vmem] * 7,
        out_specs=[
            pl.BlockSpec((1, members, slots), lambda b: (b, 0, 0)),
            pl.BlockSpec((1, INNOV_ROWS, slots), lambda b: (b, 0, 0)),
        ],
        out_shape=[
            jax.ShapeDtypeStruct((blocks, members, slots), jnp.bfloat16),
            jax.ShapeDtypeStruct((blocks, INNOV_ROWS, slots), jnp.bfloat16),
        ],
        compiler_params=pltpu.CompilerParams(vmem_limit_bytes=40 * MIB),
        cost_estimate=pl.CostEstimate(
            flops=2 * blocks * members * depth * 5 * slots,
            bytes_accessed=2 * blocks * members * (3 * depth + slots),
            transcendentals=0,
        ),
        name="gather_chosen",
    )(own, up, down, inn_own, inn_up, inn_down, picks)


def ensemble_transform(obs_rows, innov_row, obs_weight):
    count_k = obs_rows.shape[0]
    identity = jnp.eye(count_k, dtype=jnp.float32)
    weighted = (obs_rows.astype(jnp.float32) * obs_weight[None, :]).astype(jnp.bfloat16)
    precision_mat = lax.dot_general(
        weighted, obs_rows, (((1,), (1,)), ((), ())), preferred_element_type=jnp.float32
    )
    precision_mat = precision_mat + (count_k - 1.0) * identity
    trace_mean = jnp.trace(precision_mat) / count_k
    root_iter = (precision_mat / trace_mean).astype(jnp.bfloat16)
    inverse_iter = identity.astype(jnp.bfloat16)
    for repeat in range(ITERS):
        product = jnp.dot(inverse_iter, root_iter, preferred_element_type=jnp.float32)
        newton_step = (1.5 * identity - 0.5 * product).astype(jnp.bfloat16)
        if repeat + 1 < ITERS:
            root_iter = jnp.dot(root_iter, newton_step, preferred_element_type=jnp.float32).astype(
                jnp.bfloat16
            )
        inverse_iter = jnp.dot(
            newton_step, inverse_iter, preferred_element_type=jnp.float32
        ).astype(jnp.bfloat16)
    gain_vector = jnp.dot(weighted, innov_row, preferred_element_type=jnp.float32)
    inv_root = inverse_iter.astype(jnp.float32)
    inner = jnp.dot(inv_root, gain_vector, precision=lax.Precision.HIGHEST)
    mean_weight = jnp.dot(inv_root, inner, precision=lax.Precision.HIGHEST) / trace_mean
    spread_factor = jnp.sqrt((count_k - 1.0) / trace_mean)
    return (spread_factor * inv_root + mean_weight[:, None]).astype(jnp.bfloat16)


def body(
    prior_members_field,
    measure_space_deviations,
    measured_minus_predicted,
    measure_pool_indices,
    active_measure_tally,
    tapered_error_weight,
):
    place = lax.axis_index("mem")
    strips = lax.axis_size("reg")
    blocks = prior_members_field.shape[2]
    entries = prior_members_field.shape[3]
    use_count = measure_pool_indices.shape[2]
    to_next = [(i, i + 1) for i in range(strips - 1)]
    to_last = [(i + 1, i) for i in range(strips - 1)]

    def exchange(x):
        return lax.all_to_all(x, "mem", split_axis=0, concat_axis=0, tiled=True)

    obs = jnp.swapaxes(measure_space_deviations[:, 0], 0, 1)
    up = lax.ppermute(obs, "reg", to_next)
    down = lax.ppermute(obs, "reg", to_last)
    innov = measured_minus_predicted[0]
    innov_up = lax.ppermute(innov, "reg", to_next)
    innov_down = lax.ppermute(innov, "reg", to_last)

    def spread(row):
        return jnp.broadcast_to(row[:, None, :], (blocks, INNOV_ROWS, row.shape[1]))

    first = entries * 5 // 8
    state = prior_members_field[:, 0]
    state_a = exchange(jnp.swapaxes(state[:, :, :first], 0, 1))
    chosen, chosen_innov = gather_chosen(
        obs, up, down, spread(innov), spread(innov_up), spread(innov_down), measure_pool_indices[0]
    )
    state_b = jnp.swapaxes(state[:, :, first:], 0, 1)
    obs_rows = exchange(chosen)
    obs_rows, state_b = lax.optimization_barrier((obs_rows, state_b))
    state_b = exchange(state_b)
    innov_row = lax.dynamic_index_in_dim(chosen_innov[:, 0], place, 0, keepdims=False)
    obs_rows = obs_rows.reshape(-1, use_count)
    slots = jnp.arange(use_count, dtype=jnp.int32)
    obs_weight = jnp.where(slots < active_measure_tally[0, 0], tapered_error_weight[0, 0], 0.0)
    transform = ensemble_transform(obs_rows, innov_row, obs_weight)

    def analysed(part):
        shape = part.shape
        part = part.reshape(-1, shape[2]).astype(jnp.float32)
        state_mean = jnp.mean(part, axis=0)
        perturb = (part - state_mean[None, :]).astype(jnp.bfloat16)
        increment = lax.dot_general(
            transform, perturb, (((0,), (0,)), ((), ())), preferred_element_type=jnp.float32
        )
        return (state_mean[None, :] + increment).astype(jnp.bfloat16).reshape(shape)

    half = first // 2
    rest = entries - first
    parts = [
        exchange(analysed(state_a[:, :, :half])),
        exchange(analysed(state_a[:, :, half:])),
        exchange(analysed(state_b)),
    ]
    parts = [jnp.swapaxes(part, 0, 1) for part in parts]
    return jnp.concatenate(parts, axis=2)[:, None]


def solution(mesh):
    in_specs = (
        P("mem", "reg", None, None),
        P("mem", "reg", None, None),
        P("reg", None, None),
        P("reg", None, None),
        P("reg", "mem"),
        P("reg", "mem", None),
    )
    out_specs = P("mem", "reg", None, None)
    return jax.shard_map(body, mesh=mesh, in_specs=in_specs, out_specs=out_specs, check_vma=False)
```

```python
import functools

import jax
import jax.numpy as jnp
from jax import lax
from jax.experimental import pallas as pl
from jax.experimental.pallas import tpu as pltpu
from jax.sharding import PartitionSpec as P

ITERS = 2
INNOV_ROWS = 16
SLOT_CHUNK = 256
MEMBER_TILE = 32
MIB = 1024 * 1024


def gather_kernel(own_ref, up_ref, down_ref, inn_own, inn_up, inn_down, idx_ref, out_ref, inn_ref):
    block = pl.program_id(0)
    blocks = own_ref.shape[0]
    depth = own_ref.shape[2]
    members = own_ref.shape[1]
    west = jnp.maximum(block - 1, 0)
    east = jnp.minimum(block + 1, blocks - 1)
    slots = out_ref.shape[2]
    sources = (
        (own_ref, inn_own, block, None),
        (up_ref, inn_up, block, None),
        (down_ref, inn_down, block, None),
        (own_ref, inn_own, west, block > 0),
        (own_ref, inn_own, east, block < blocks - 1),
    )
    rows = lax.broadcasted_iota(jnp.int32, (depth, SLOT_CHUNK), 0)

    @pl.loop(0, slots // SLOT_CHUNK)
    def _(chunk):
        where = pl.ds(pl.multiple_of(chunk * SLOT_CHUNK, SLOT_CHUNK), SLOT_CHUNK)
        picks = idx_ref[pl.ds(block, 1), where]
        acc = jnp.zeros((members + INNOV_ROWS, SLOT_CHUNK), jnp.float32)
        for number, (ref, inn, at, live) in enumerate(sources):
            local = picks - number * depth
            if live is not None:
                local = jnp.where(live, local, -1)
            one_hot = jnp.where(rows == local, 1.0, 0.0).astype(jnp.bfloat16)
            lhs = jnp.concatenate([ref[at], inn[at]], axis=0)
            acc += jnp.dot(lhs, one_hot, preferred_element_type=jnp.float32)
        out_ref[0, :, where] = acc[:members].astype(jnp.bfloat16)
        inn_ref[0, :, where] = acc[members:].astype(jnp.bfloat16)


def gather_chosen(own, up, down, inn_own, inn_up, inn_down, picks):
    blocks, members, depth = own.shape
    slots = picks.shape[1]
    vmem = pl.BlockSpec(memory_space=pltpu.VMEM)
    return pl.pallas_call(
        gather_kernel,
        grid=(blocks,),
        in_specs=[vmem] * 7,
        out_specs=[
            pl.BlockSpec((1, members, slots), lambda b: (b, 0, 0)),
            pl.BlockSpec((1, INNOV_ROWS, slots), lambda b: (b, 0, 0)),
        ],
        out_shape=[
            jax.ShapeDtypeStruct((blocks, members, slots), jnp.bfloat16),
            jax.ShapeDtypeStruct((blocks, INNOV_ROWS, slots), jnp.bfloat16),
        ],
        compiler_params=pltpu.CompilerParams(vmem_limit_bytes=40 * MIB),
        cost_estimate=pl.CostEstimate(
            flops=2 * blocks * members * depth * 5 * slots,
            bytes_accessed=2 * blocks * members * (3 * depth + slots),
            transcendentals=0,
        ),
        name="gather_chosen",
    )(own, up, down, inn_own, inn_up, inn_down, picks)


def to_blocks_kernel(in_ref, out_ref):
    out_ref[...] = jnp.swapaxes(in_ref[...], 0, 1)


def to_blocks(state, start, width, name):
    members, blocks, _ = state.shape
    return pl.pallas_call(
        to_blocks_kernel,
        grid=(members // MEMBER_TILE,),
        in_specs=[
            pl.BlockSpec((MEMBER_TILE, blocks, pl.Element(width)), lambda i: (i, 0, start))
            if start % width
            else pl.BlockSpec((MEMBER_TILE, blocks, width), lambda i: (i, 0, start // width))
        ],
        out_specs=pl.BlockSpec((blocks, MEMBER_TILE, width), lambda i: (0, i, 0)),
        out_shape=jax.ShapeDtypeStruct((blocks, members, width), state.dtype),
        compiler_params=pltpu.CompilerParams(vmem_limit_bytes=32 * MIB),
        cost_estimate=pl.CostEstimate(
            flops=0, bytes_accessed=4 * members * blocks * width, transcendentals=0
        ),
        name=name,
    )(state)


def to_members_kernel(part_ref, *refs):
    refs[-1][...] = jnp.swapaxes(part_ref[...], 0, 1)


def to_members(part, start, entries, whole, name):
    blocks, members, width = part.shape
    before = [] if whole is None else [whole]
    return pl.pallas_call(
        to_members_kernel,
        grid=(members // MEMBER_TILE,),
        in_specs=[pl.BlockSpec((blocks, MEMBER_TILE, width), lambda i: (0, i, 0))]
        + [pl.BlockSpec(memory_space=pl.ANY)] * len(before),
        out_specs=pl.BlockSpec((MEMBER_TILE, blocks, width), lambda i: (i, 0, start // width)),
        out_shape=jax.ShapeDtypeStruct((members, blocks, entries), part.dtype),
        input_output_aliases={1: 0} if before else {},
        compiler_params=pltpu.CompilerParams(vmem_limit_bytes=32 * MIB),
        cost_estimate=pl.CostEstimate(
            flops=0, bytes_accessed=4 * members * blocks * width, transcendentals=0
        ),
        name=name,
    )(part, *before)


def ensemble_transform(obs_rows, innov_row, obs_weight):
    count_k = obs_rows.shape[0]
    identity = jnp.eye(count_k, dtype=jnp.float32)
    weighted = (obs_rows.astype(jnp.float32) * obs_weight[None, :]).astype(jnp.bfloat16)
    precision_mat = lax.dot_general(
        weighted, obs_rows, (((1,), (1,)), ((), ())), preferred_element_type=jnp.float32
    )
    precision_mat = precision_mat + (count_k - 1.0) * identity
    trace_mean = jnp.trace(precision_mat) / count_k
    root_iter = (precision_mat / trace_mean).astype(jnp.bfloat16)
    inverse_iter = identity.astype(jnp.bfloat16)
    for repeat in range(ITERS):
        product = jnp.dot(inverse_iter, root_iter, preferred_element_type=jnp.float32)
        newton_step = (1.5 * identity - 0.5 * product).astype(jnp.bfloat16)
        if repeat + 1 < ITERS:
            root_iter = jnp.dot(root_iter, newton_step, preferred_element_type=jnp.float32).astype(
                jnp.bfloat16
            )
        inverse_iter = jnp.dot(
            newton_step, inverse_iter, preferred_element_type=jnp.float32
        ).astype(jnp.bfloat16)
    gain_vector = jnp.dot(weighted, innov_row, preferred_element_type=jnp.float32)
    inv_root = inverse_iter.astype(jnp.float32)
    inner = jnp.dot(inv_root, gain_vector, precision=lax.Precision.HIGHEST)
    mean_weight = jnp.dot(inv_root, inner, precision=lax.Precision.HIGHEST) / trace_mean
    spread_factor = jnp.sqrt((count_k - 1.0) / trace_mean)
    return (spread_factor * inv_root + mean_weight[:, None]).astype(jnp.bfloat16)


def body(
    prior_members_field,
    measure_space_deviations,
    measured_minus_predicted,
    measure_pool_indices,
    active_measure_tally,
    tapered_error_weight,
):
    place = lax.axis_index("mem")
    strips = lax.axis_size("reg")
    blocks = prior_members_field.shape[2]
    entries = prior_members_field.shape[3]
    use_count = measure_pool_indices.shape[2]
    to_next = [(i, i + 1) for i in range(strips - 1)]
    to_last = [(i + 1, i) for i in range(strips - 1)]

    def exchange(x):
        return lax.all_to_all(x, "mem", split_axis=0, concat_axis=0, tiled=True)

    obs = jnp.swapaxes(measure_space_deviations[:, 0], 0, 1)
    up = lax.ppermute(obs, "reg", to_next)
    down = lax.ppermute(obs, "reg", to_last)
    innov = measured_minus_predicted[0]
    innov_up = lax.ppermute(innov, "reg", to_next)
    innov_down = lax.ppermute(innov, "reg", to_last)

    def spread(row):
        return jnp.broadcast_to(row[:, None, :], (blocks, INNOV_ROWS, row.shape[1]))

    width = entries // 4
    state = prior_members_field[:, 0]
    state_a = exchange(to_blocks(state, 0, 2 * width, "state_a"))
    chosen, chosen_innov = gather_chosen(
        obs, up, down, spread(innov), spread(innov_up), spread(innov_down), measure_pool_indices[0]
    )
    state_b = to_blocks(state, 2 * width, 2 * width, "state_b")
    obs_rows = exchange(chosen)
    obs_rows, state_b = lax.optimization_barrier((obs_rows, state_b))
    state_b = exchange(state_b)
    innov_row = lax.dynamic_index_in_dim(chosen_innov[:, 0], place, 0, keepdims=False)
    obs_rows = obs_rows.reshape(-1, use_count)
    slots = jnp.arange(use_count, dtype=jnp.int32)
    obs_weight = jnp.where(slots < active_measure_tally[0, 0], tapered_error_weight[0, 0], 0.0)
    transform = ensemble_transform(obs_rows, innov_row, obs_weight)

    def analysed(part):
        shape = part.shape
        part = part.reshape(-1, shape[2]).astype(jnp.float32)
        state_mean = jnp.mean(part, axis=0)
        perturb = (part - state_mean[None, :]).astype(jnp.bfloat16)
        increment = lax.dot_general(
            transform, perturb, (((0,), (0,)), ((), ())), preferred_element_type=jnp.float32
        )
        return (state_mean[None, :] + increment).astype(jnp.bfloat16).reshape(shape)

    done_a = analysed(state_a)
    done_a, state_b = lax.optimization_barrier((done_a, state_b))
    done_a = exchange(done_a)
    done_b = exchange(analysed(state_b))
    whole = to_members(done_a, 0, entries, None, "analysis_a")
    whole = to_members(done_b, 2 * width, entries, whole, "analysis_b")
    return whole[:, None]


def solution(mesh):
    in_specs = (
        P("mem", "reg", None, None),
        P("mem", "reg", None, None),
        P("reg", None, None),
        P("reg", None, None),
        P("reg", "mem"),
        P("reg", "mem", None),
    )
    out_specs = P("mem", "reg", None, None)
    return jax.shard_map(body, mesh=mesh, in_specs=in_specs, out_specs=out_specs, check_vma=False)
```

```python
import functools

import jax
import jax.numpy as jnp
from jax import lax
from jax.experimental import pallas as pl
from jax.experimental.pallas import tpu as pltpu
from jax.sharding import PartitionSpec as P

INNOV_ROWS = 16
SLOT_CHUNK = 256
MEMBER_TILE = 32
TRANSFORM_CHUNK = 256
ANALYSIS_TILE = 256
MIB = 1024 * 1024


def gather_kernel(own_ref, up_ref, down_ref, inn_own, inn_up, inn_down, idx_ref, out_ref, inn_ref):
    block = pl.program_id(0)
    blocks = own_ref.shape[0]
    depth = own_ref.shape[2]
    members = own_ref.shape[1]
    west = jnp.maximum(block - 1, 0)
    east = jnp.minimum(block + 1, blocks - 1)
    slots = out_ref.shape[2]
    sources = (
        (own_ref, inn_own, block, None),
        (up_ref, inn_up, block, None),
        (down_ref, inn_down, block, None),
        (own_ref, inn_own, west, block > 0),
        (own_ref, inn_own, east, block < blocks - 1),
    )
    rows = lax.broadcasted_iota(jnp.int32, (depth, SLOT_CHUNK), 0)

    @pl.loop(0, slots // SLOT_CHUNK)
    def _(chunk):
        where = pl.ds(pl.multiple_of(chunk * SLOT_CHUNK, SLOT_CHUNK), SLOT_CHUNK)
        picks = idx_ref[pl.ds(block, 1), where]
        acc = jnp.zeros((members + INNOV_ROWS, SLOT_CHUNK), jnp.float32)
        for number, (ref, inn, at, live) in enumerate(sources):
            local = picks - number * depth
            if live is not None:
                local = jnp.where(live, local, -1)
            one_hot = jnp.where(rows == local, 1.0, 0.0).astype(jnp.bfloat16)
            lhs = jnp.concatenate([ref[at], inn[at]], axis=0)
            acc += jnp.dot(lhs, one_hot, preferred_element_type=jnp.float32)
        out_ref[0, :, where] = acc[:members].astype(jnp.bfloat16)
        inn_ref[0, :, where] = acc[members:].astype(jnp.bfloat16)


def gather_chosen(own, up, down, inn_own, inn_up, inn_down, picks):
    blocks, members, depth = own.shape
    slots = picks.shape[1]
    vmem = pl.BlockSpec(memory_space=pltpu.VMEM)
    return pl.pallas_call(
        gather_kernel,
        grid=(blocks,),
        in_specs=[vmem] * 7,
        out_specs=[
            pl.BlockSpec((1, members, slots), lambda b: (b, 0, 0)),
            pl.BlockSpec((1, INNOV_ROWS, slots), lambda b: (b, 0, 0)),
        ],
        out_shape=[
            jax.ShapeDtypeStruct((blocks, members, slots), jnp.bfloat16),
            jax.ShapeDtypeStruct((blocks, INNOV_ROWS, slots), jnp.bfloat16),
        ],
        compiler_params=pltpu.CompilerParams(vmem_limit_bytes=40 * MIB),
        cost_estimate=pl.CostEstimate(
            flops=2 * blocks * members * depth * 5 * slots,
            bytes_accessed=2 * blocks * members * (3 * depth + slots),
            transcendentals=0,
        ),
        name="gather_chosen",
    )(own, up, down, inn_own, inn_up, inn_down, picks)


def to_blocks_kernel(in_ref, out_ref):
    out_ref[...] = jnp.swapaxes(in_ref[...], 0, 1)


def to_blocks(state, start, width, name):
    members, blocks, _ = state.shape
    return pl.pallas_call(
        to_blocks_kernel,
        grid=(members // MEMBER_TILE,),
        in_specs=[
            pl.BlockSpec((MEMBER_TILE, blocks, pl.Element(width)), lambda i: (i, 0, start))
            if start % width
            else pl.BlockSpec((MEMBER_TILE, blocks, width), lambda i: (i, 0, start // width))
        ],
        out_specs=pl.BlockSpec((blocks, MEMBER_TILE, width), lambda i: (0, i, 0)),
        out_shape=jax.ShapeDtypeStruct((blocks, members, width), state.dtype),
        compiler_params=pltpu.CompilerParams(vmem_limit_bytes=32 * MIB),
        cost_estimate=pl.CostEstimate(
            flops=0, bytes_accessed=4 * members * blocks * width, transcendentals=0
        ),
        name=name,
    )(state)


def to_members_kernel(part_ref, *refs):
    refs[-1][...] = jnp.swapaxes(part_ref[...], 0, 1)


def to_members(part, start, entries, whole, name):
    blocks, members, width = part.shape
    before = [] if whole is None else [whole]
    return pl.pallas_call(
        to_members_kernel,
        grid=(members // MEMBER_TILE,),
        in_specs=[pl.BlockSpec((blocks, MEMBER_TILE, width), lambda i: (0, i, 0))]
        + [pl.BlockSpec(memory_space=pl.ANY)] * len(before),
        out_specs=pl.BlockSpec((MEMBER_TILE, blocks, width), lambda i: (i, 0, start // width)),
        out_shape=jax.ShapeDtypeStruct((members, blocks, entries), part.dtype),
        input_output_aliases={1: 0} if before else {},
        compiler_params=pltpu.CompilerParams(vmem_limit_bytes=32 * MIB),
        cost_estimate=pl.CostEstimate(
            flops=0, bytes_accessed=4 * members * blocks * width, transcendentals=0
        ),
        name=name,
    )(part, *before)


def transform_kernel(
    tally_ref, weight_ref, innov_ref, obs_ref, out_ref,
    weighted, precision, root, step, root_next, step_next, inverse,
):
    count_k, slots = obs_ref.shape
    spare = count_k - 1.0
    chunks = count_k // TRANSFORM_CHUNK
    live = lax.broadcasted_iota(jnp.int32, (1, slots), 1) < tally_ref[0, 0]
    obs_weight = jnp.where(live, weight_ref[...], 0.0)

    def span(chunk):
        return pl.ds(pl.multiple_of(chunk * TRANSFORM_CHUNK, TRANSFORM_CHUNK), TRANSFORM_CHUNK)

    def on_diagonal(chunk, value):
        rows = lax.broadcasted_iota(jnp.int32, (count_k, TRANSFORM_CHUNK), 0)
        columns = lax.broadcasted_iota(jnp.int32, (count_k, TRANSFORM_CHUNK), 1)
        return jnp.where(rows == columns + chunk * TRANSFORM_CHUNK, value, 0.0)

    def matmul(left, right):
        return jnp.dot(left, right, preferred_element_type=jnp.float32)

    def by_rows(left, right):
        return lax.dot_general(
            left, right, (((1,), (1,)), ((), ())), preferred_element_type=jnp.float32
        )

    def precise(row, matrix):
        high = row.astype(jnp.bfloat16)
        rest = row - high.astype(jnp.float32)
        middle = rest.astype(jnp.bfloat16)
        low = (rest - middle.astype(jnp.float32)).astype(jnp.bfloat16)
        return (matmul(low, matrix) + matmul(middle, matrix)) + matmul(high, matrix)

    def weigh(chunk, trace):
        at = span(chunk)
        scaled = (obs_ref[at, :].astype(jnp.float32) * obs_weight).astype(jnp.bfloat16)
        weighted[at, :] = scaled
        product = by_rows(obs_ref[...], scaled)
        precision[:, at] = product
        return trace + jnp.sum(on_diagonal(chunk, product))

    trace = lax.fori_loop(0, chunks, weigh, jnp.float32(0.0))
    trace_mean = trace / count_k + spare
    scale = 1.0 / trace_mean
    gain = by_rows(innov_ref[...], weighted[...])

    @pl.loop(0, chunks)
    def _(chunk):
        at = span(chunk)
        first = ((precision[:, at] + on_diagonal(chunk, spare)) * scale).astype(jnp.bfloat16)
        root[:, at] = first
        step[:, at] = (on_diagonal(chunk, 1.5) - 0.5 * first.astype(jnp.float32)).astype(jnp.bfloat16)

    @pl.loop(0, chunks)
    def _(chunk):
        at = span(chunk)
        root_next[:, at] = matmul(step[...], root[:, at]).astype(jnp.bfloat16)

    @pl.loop(0, chunks)
    def _(chunk):
        at = span(chunk)
        product = matmul(root_next[...], step[:, at])
        step_next[:, at] = (on_diagonal(chunk, 1.5) - 0.5 * product).astype(jnp.bfloat16)

    @pl.loop(0, chunks)
    def _(chunk):
        at = span(chunk)
        inverse[:, at] = matmul(step[...], step_next[:, at]).astype(jnp.bfloat16)

    inner = precise(gain, inverse[...])
    mean_weight = precise(inner, inverse[...])[:1] * scale
    spread_factor = jnp.sqrt(jnp.full((1, slots), spare * scale, jnp.float32))
    out_ref[...] = (
        spread_factor[:, :count_k] * inverse[...].astype(jnp.float32) + mean_weight
    ).astype(jnp.bfloat16)


def ensemble_transform(tally, weight, innov, obs_rows):
    count_k, slots = obs_rows.shape
    vmem = pl.BlockSpec(memory_space=pltpu.VMEM)
    square = pltpu.VMEM((count_k, count_k), jnp.bfloat16)
    return pl.pallas_call(
        transform_kernel,
        in_specs=[pl.BlockSpec(memory_space=pltpu.SMEM), vmem, vmem, vmem],
        out_specs=vmem,
        out_shape=jax.ShapeDtypeStruct((count_k, count_k), jnp.bfloat16),
        scratch_shapes=[
            pltpu.VMEM((count_k, slots), jnp.bfloat16),
            pltpu.VMEM((count_k, count_k), jnp.float32),
            square, square, square, square, square,
        ],
        compiler_params=pltpu.CompilerParams(vmem_limit_bytes=40 * MIB),
        cost_estimate=pl.CostEstimate(
            flops=2 * count_k * count_k * (slots + 3 * count_k),
            bytes_accessed=4 * count_k * (slots + count_k),
            transcendentals=0,
        ),
        name="transform",
    )(tally, weight, innov, obs_rows)


def analysis_kernel(transform_ref, state_ref, out_ref):
    state = state_ref[...].astype(jnp.float32)
    state_mean = jnp.sum(state, axis=0, keepdims=True) * (1.0 / state.shape[0])
    perturb = (state - state_mean).astype(jnp.bfloat16)
    increment = jnp.dot(transform_ref[...], perturb, preferred_element_type=jnp.float32)
    out_ref[...] = (state_mean + increment).astype(jnp.bfloat16)


def analysed(transform, part, name):
    blocks, members, width = part.shape
    count_k = blocks * members
    out = pl.pallas_call(
        analysis_kernel,
        grid=(width // ANALYSIS_TILE,),
        in_specs=[
            pl.BlockSpec(memory_space=pltpu.VMEM),
            pl.BlockSpec((count_k, ANALYSIS_TILE), lambda i: (0, i)),
        ],
        out_specs=pl.BlockSpec((count_k, ANALYSIS_TILE), lambda i: (0, i)),
        out_shape=jax.ShapeDtypeStruct((count_k, width), jnp.bfloat16),
        compiler_params=pltpu.CompilerParams(vmem_limit_bytes=32 * MIB),
        cost_estimate=pl.CostEstimate(
            flops=2 * count_k * count_k * width,
            bytes_accessed=2 * count_k * (2 * width + count_k),
            transcendentals=0,
        ),
        name=name,
    )(transform, part.reshape(count_k, width))
    return out.reshape(part.shape)


def body(
    prior_members_field,
    measure_space_deviations,
    measured_minus_predicted,
    measure_pool_indices,
    active_measure_tally,
    tapered_error_weight,
):
    place = lax.axis_index("mem")
    strips = lax.axis_size("reg")
    blocks = prior_members_field.shape[2]
    entries = prior_members_field.shape[3]
    use_count = measure_pool_indices.shape[2]
    to_next = [(i, i + 1) for i in range(strips - 1)]
    to_last = [(i + 1, i) for i in range(strips - 1)]

    def exchange(x):
        return lax.all_to_all(x, "mem", split_axis=0, concat_axis=0, tiled=True)

    obs = jnp.swapaxes(measure_space_deviations[:, 0], 0, 1)
    up = lax.ppermute(obs, "reg", to_next)
    down = lax.ppermute(obs, "reg", to_last)
    innov = measured_minus_predicted[0]
    innov_up = lax.ppermute(innov, "reg", to_next)
    innov_down = lax.ppermute(innov, "reg", to_last)

    def spread(row):
        return jnp.broadcast_to(row[:, None, :], (blocks, INNOV_ROWS, row.shape[1]))

    quarter = entries // 4
    state = prior_members_field[:, 0]
    state_a = exchange(to_blocks(state, 0, 2 * quarter, "state_a"))
    chosen, chosen_innov = gather_chosen(
        obs, up, down, spread(innov), spread(innov_up), spread(innov_down), measure_pool_indices[0]
    )
    state_b = to_blocks(state, 2 * quarter, 2 * quarter, "state_b")
    obs_rows = exchange(chosen)
    obs_rows, state_b = lax.optimization_barrier((obs_rows, state_b))
    state_b = exchange(state_b)
    innov_rows = lax.dynamic_index_in_dim(chosen_innov, place, 0, keepdims=False)
    transform = ensemble_transform(
        active_measure_tally, tapered_error_weight[0], innov_rows, obs_rows.reshape(-1, use_count)
    )
    done_a = analysed(transform, state_a, "analysed_a")
    done_a, state_b = lax.optimization_barrier((done_a, state_b))
    done_a = exchange(done_a)
    done_b = exchange(analysed(transform, state_b, "analysed_b"))
    whole = to_members(done_a, 0, entries, None, "analysis_a")
    whole = to_members(done_b, 2 * quarter, entries, whole, "analysis_b")
    return whole[:, None]


def solution(mesh):
    in_specs = (
        P("mem", "reg", None, None),
        P("mem", "reg", None, None),
        P("reg", None, None),
        P("reg", None, None),
        P("reg", "mem"),
        P("reg", "mem", None),
    )
    out_specs = P("mem", "reg", None, None)
    return jax.shard_map(body, mesh=mesh, in_specs=in_specs, out_specs=out_specs, check_vma=False)
```

```python
import functools

import jax
import jax.numpy as jnp
from jax import lax
from jax.experimental import pallas as pl
from jax.experimental.pallas import tpu as pltpu
from jax.sharding import PartitionSpec as P

INNOV_ROWS = 16
SLOT_CHUNK = 256
MEMBER_TILE = 32
POOL_TILE = 256
TRANSFORM_CHUNK = 256
ANALYSIS_TILE = 256
MIB = 1024 * 1024


def pool_kernel(obs_ref, innov_ref, out_ref):
    members = obs_ref.shape[0]
    out_ref[:, :members, :] = jnp.swapaxes(obs_ref[...], 0, 1)
    shape = (out_ref.shape[0], INNOV_ROWS, out_ref.shape[2])
    out_ref[:, members:, :] = jnp.broadcast_to(innov_ref[...][:, None, :], shape)


def pool_rows(obs, innov):
    members, blocks, depth = obs.shape
    rows = members + INNOV_ROWS
    return pl.pallas_call(
        pool_kernel,
        grid=(depth // POOL_TILE,),
        in_specs=[
            pl.BlockSpec((members, blocks, POOL_TILE), lambda i: (0, 0, i)),
            pl.BlockSpec((blocks, POOL_TILE), lambda i: (0, i)),
        ],
        out_specs=pl.BlockSpec((blocks, rows, POOL_TILE), lambda i: (0, 0, i)),
        out_shape=jax.ShapeDtypeStruct((blocks, rows, depth), obs.dtype),
        compiler_params=pltpu.CompilerParams(vmem_limit_bytes=60 * MIB),
        cost_estimate=pl.CostEstimate(
            flops=0, bytes_accessed=4 * rows * blocks * depth, transcendentals=0
        ),
        name="pool_rows",
    )(obs, innov)


def gather_kernel(own_ref, up_ref, down_ref, idx_ref, out_ref, inn_ref):
    block = pl.program_id(0)
    blocks, rows, depth = own_ref.shape
    members = out_ref.shape[1]
    slots = out_ref.shape[2]
    west = jnp.maximum(block - 1, 0)
    east = jnp.minimum(block + 1, blocks - 1)
    sources = (
        (own_ref, block, None),
        (up_ref, block, None),
        (down_ref, block, None),
        (own_ref, west, block > 0),
        (own_ref, east, block < blocks - 1),
    )
    columns = lax.broadcasted_iota(jnp.int32, (depth, SLOT_CHUNK), 0)

    @pl.loop(0, slots // SLOT_CHUNK)
    def _(chunk):
        where = pl.ds(pl.multiple_of(chunk * SLOT_CHUNK, SLOT_CHUNK), SLOT_CHUNK)
        picks = idx_ref[pl.ds(block, 1), where]
        acc = jnp.zeros((rows, SLOT_CHUNK), jnp.float32)
        for number, (ref, at, live) in enumerate(sources):
            local = picks - number * depth
            if live is not None:
                local = jnp.where(live, local, -1)
            one_hot = jnp.where(columns == local, 1.0, 0.0).astype(jnp.bfloat16)
            acc += jnp.dot(ref[at], one_hot, preferred_element_type=jnp.float32)
        out_ref[0, :, where] = acc[:members].astype(jnp.bfloat16)
        inn_ref[0, :, where] = acc[members:].astype(jnp.bfloat16)


def gather_chosen(own, up, down, picks):
    blocks, rows, depth = own.shape
    members = rows - INNOV_ROWS
    slots = picks.shape[1]
    vmem = pl.BlockSpec(memory_space=pltpu.VMEM)
    return pl.pallas_call(
        gather_kernel,
        grid=(blocks,),
        in_specs=[vmem] * 4,
        out_specs=[
            pl.BlockSpec((1, members, slots), lambda b: (b, 0, 0)),
            pl.BlockSpec((1, INNOV_ROWS, slots), lambda b: (b, 0, 0)),
        ],
        out_shape=[
            jax.ShapeDtypeStruct((blocks, members, slots), jnp.bfloat16),
            jax.ShapeDtypeStruct((blocks, INNOV_ROWS, slots), jnp.bfloat16),
        ],
        compiler_params=pltpu.CompilerParams(vmem_limit_bytes=40 * MIB),
        cost_estimate=pl.CostEstimate(
            flops=2 * blocks * rows * depth * 5 * slots,
            bytes_accessed=2 * blocks * rows * (3 * depth + slots),
            transcendentals=0,
        ),
        name="gather_chosen",
    )(own, up, down, picks)


def to_blocks_kernel(in_ref, out_ref):
    out_ref[...] = jnp.swapaxes(in_ref[...], 0, 1)


def to_blocks(state, start, width, name):
    members, blocks, _ = state.shape
    return pl.pallas_call(
        to_blocks_kernel,
        grid=(members // MEMBER_TILE,),
        in_specs=[
            pl.BlockSpec((MEMBER_TILE, blocks, pl.Element(width)), lambda i: (i, 0, start))
            if start % width
            else pl.BlockSpec((MEMBER_TILE, blocks, width), lambda i: (i, 0, start // width))
        ],
        out_specs=pl.BlockSpec((blocks, MEMBER_TILE, width), lambda i: (0, i, 0)),
        out_shape=jax.ShapeDtypeStruct((blocks, members, width), state.dtype),
        compiler_params=pltpu.CompilerParams(vmem_limit_bytes=60 * MIB),
        cost_estimate=pl.CostEstimate(
            flops=0, bytes_accessed=4 * members * blocks * width, transcendentals=0
        ),
        name=name,
    )(state)


def to_members_kernel(part_ref, *refs):
    refs[-1][...] = jnp.swapaxes(part_ref[...], 0, 1)


def to_members(part, start, entries, whole, name):
    blocks, members, width = part.shape
    before = [] if whole is None else [whole]
    return pl.pallas_call(
        to_members_kernel,
        grid=(members // MEMBER_TILE,),
        in_specs=[pl.BlockSpec((blocks, MEMBER_TILE, width), lambda i: (0, i, 0))]
        + [pl.BlockSpec(memory_space=pl.ANY)] * len(before),
        out_specs=pl.BlockSpec((MEMBER_TILE, blocks, width), lambda i: (i, 0, start // width)),
        out_shape=jax.ShapeDtypeStruct((members, blocks, entries), part.dtype),
        input_output_aliases={1: 0} if before else {},
        compiler_params=pltpu.CompilerParams(vmem_limit_bytes=32 * MIB),
        cost_estimate=pl.CostEstimate(
            flops=0, bytes_accessed=4 * members * blocks * width, transcendentals=0
        ),
        name=name,
    )(part, *before)


def transform_kernel(
    tally_ref, weight_ref, innov_ref, obs_ref, out_ref,
    weighted, precision, root, step, root_next, step_next, inverse,
):
    count_k, slots = obs_ref.shape
    spare = count_k - 1.0
    chunks = count_k // TRANSFORM_CHUNK
    live = lax.broadcasted_iota(jnp.int32, (1, slots), 1) < tally_ref[0, 0]
    obs_weight = jnp.where(live, weight_ref[...], 0.0)

    def span(chunk):
        return pl.ds(pl.multiple_of(chunk * TRANSFORM_CHUNK, TRANSFORM_CHUNK), TRANSFORM_CHUNK)

    def on_diagonal(chunk, value):
        rows = lax.broadcasted_iota(jnp.int32, (count_k, TRANSFORM_CHUNK), 0)
        columns = lax.broadcasted_iota(jnp.int32, (count_k, TRANSFORM_CHUNK), 1)
        return jnp.where(rows == columns + chunk * TRANSFORM_CHUNK, value, 0.0)

    def matmul(left, right):
        return jnp.dot(left, right, preferred_element_type=jnp.float32)

    def by_rows(left, right):
        return lax.dot_general(
            left, right, (((1,), (1,)), ((), ())), preferred_element_type=jnp.float32
        )

    def precise(row, matrix):
        high = row.astype(jnp.bfloat16)
        rest = row - high.astype(jnp.float32)
        middle = rest.astype(jnp.bfloat16)
        low = (rest - middle.astype(jnp.float32)).astype(jnp.bfloat16)
        return (matmul(low, matrix) + matmul(middle, matrix)) + matmul(high, matrix)

    def weigh(chunk, trace):
        at = span(chunk)
        scaled = (obs_ref[at, :].astype(jnp.float32) * obs_weight).astype(jnp.bfloat16)
        weighted[at, :] = scaled
        product = by_rows(obs_ref[...], scaled)
        precision[:, at] = product
        return trace + jnp.sum(on_diagonal(chunk, product))

    trace = lax.fori_loop(0, chunks, weigh, jnp.float32(0.0))
    trace_mean = trace / count_k + spare
    scale = 1.0 / trace_mean
    gain = by_rows(innov_ref[...], weighted[...])

    @pl.loop(0, chunks)
    def _(chunk):
        at = span(chunk)
        first = ((precision[:, at] + on_diagonal(chunk, spare)) * scale).astype(jnp.bfloat16)
        root[:, at] = first
        step[:, at] = (on_diagonal(chunk, 1.5) - 0.5 * first.astype(jnp.float32)).astype(jnp.bfloat16)

    @pl.loop(0, chunks)
    def _(chunk):
        at = span(chunk)
        root_next[:, at] = matmul(step[...], root[:, at]).astype(jnp.bfloat16)

    @pl.loop(0, chunks)
    def _(chunk):
        at = span(chunk)
        product = matmul(root_next[...], step[:, at])
        step_next[:, at] = (on_diagonal(chunk, 1.5) - 0.5 * product).astype(jnp.bfloat16)

    @pl.loop(0, chunks)
    def _(chunk):
        at = span(chunk)
        inverse[:, at] = matmul(step[...], step_next[:, at]).astype(jnp.bfloat16)

    inner = precise(gain, inverse[...])
    mean_weight = precise(inner, inverse[...])[:1] * scale
    spread_factor = jnp.sqrt(jnp.full((1, slots), spare * scale, jnp.float32))
    out_ref[...] = (
        spread_factor[:, :count_k] * inverse[...].astype(jnp.float32) + mean_weight
    ).astype(jnp.bfloat16)


def ensemble_transform(tally, weight, innov, obs_rows):
    count_k, slots = obs_rows.shape
    vmem = pl.BlockSpec(memory_space=pltpu.VMEM)
    square = pltpu.VMEM((count_k, count_k), jnp.bfloat16)
    return pl.pallas_call(
        transform_kernel,
        in_specs=[pl.BlockSpec(memory_space=pltpu.SMEM), vmem, vmem, vmem],
        out_specs=vmem,
        out_shape=jax.ShapeDtypeStruct((count_k, count_k), jnp.bfloat16),
        scratch_shapes=[
            pltpu.VMEM((count_k, slots), jnp.bfloat16),
            pltpu.VMEM((count_k, count_k), jnp.float32),
            square, square, square, square, square,
        ],
        compiler_params=pltpu.CompilerParams(vmem_limit_bytes=40 * MIB),
        cost_estimate=pl.CostEstimate(
            flops=2 * count_k * count_k * (slots + 3 * count_k),
            bytes_accessed=4 * count_k * (slots + count_k),
            transcendentals=0,
        ),
        name="transform",
    )(tally, weight, innov, obs_rows)


def analysis_kernel(transform_ref, state_ref, out_ref):
    state = state_ref[...].astype(jnp.float32)
    state_mean = jnp.sum(state, axis=0, keepdims=True) * (1.0 / state.shape[0])
    perturb = (state - state_mean).astype(jnp.bfloat16)
    increment = jnp.dot(transform_ref[...], perturb, preferred_element_type=jnp.float32)
    out_ref[...] = (state_mean + increment).astype(jnp.bfloat16)


def analysed(transform, part, name):
    blocks, members, width = part.shape
    count_k = blocks * members
    out = pl.pallas_call(
        analysis_kernel,
        grid=(width // ANALYSIS_TILE,),
        in_specs=[
            pl.BlockSpec(memory_space=pltpu.VMEM),
            pl.BlockSpec((count_k, ANALYSIS_TILE), lambda i: (0, i)),
        ],
        out_specs=pl.BlockSpec((count_k, ANALYSIS_TILE), lambda i: (0, i)),
        out_shape=jax.ShapeDtypeStruct((count_k, width), jnp.bfloat16),
        compiler_params=pltpu.CompilerParams(vmem_limit_bytes=32 * MIB),
        cost_estimate=pl.CostEstimate(
            flops=2 * count_k * count_k * width,
            bytes_accessed=2 * count_k * (2 * width + count_k),
            transcendentals=0,
        ),
        name=name,
    )(transform, part.reshape(count_k, width))
    return out.reshape(part.shape)


def body(
    prior_members_field,
    measure_space_deviations,
    measured_minus_predicted,
    measure_pool_indices,
    active_measure_tally,
    tapered_error_weight,
):
    place = lax.axis_index("mem")
    strips = lax.axis_size("reg")
    blocks = prior_members_field.shape[2]
    entries = prior_members_field.shape[3]
    use_count = measure_pool_indices.shape[2]
    to_next = [(i, i + 1) for i in range(strips - 1)]
    to_last = [(i + 1, i) for i in range(strips - 1)]

    def exchange(x):
        return lax.all_to_all(x, "mem", split_axis=0, concat_axis=0, tiled=True)

    quarter = entries // 4
    state = prior_members_field[:, 0]
    state_a = to_blocks(state, 0, 2 * quarter, "state_a")
    devs, state_a = lax.optimization_barrier((measure_space_deviations[:, 0], state_a))
    state_a = exchange(state_a)
    pool = pool_rows(devs, measured_minus_predicted[0])
    up = lax.ppermute(pool, "reg", to_next)
    down = lax.ppermute(pool, "reg", to_last)
    chosen, chosen_innov = gather_chosen(pool, up, down, measure_pool_indices[0])
    chosen, state_a = lax.optimization_barrier((chosen, state_a))
    obs_rows = exchange(chosen)
    state_b = to_blocks(state, 2 * quarter, 2 * quarter, "state_b")
    obs_rows, state_b = lax.optimization_barrier((obs_rows, state_b))
    state_b = exchange(state_b)
    innov_rows = lax.dynamic_index_in_dim(chosen_innov, place, 0, keepdims=False)
    transform = ensemble_transform(
        active_measure_tally, tapered_error_weight[0], innov_rows, obs_rows.reshape(-1, use_count)
    )
    done_a = analysed(transform, state_a, "analysed_a")
    done_a, state_b = lax.optimization_barrier((done_a, state_b))
    done_a = exchange(done_a)
    done_b = exchange(analysed(transform, state_b, "analysed_b"))
    whole = to_members(done_a, 0, entries, None, "analysis_a")
    whole = to_members(done_b, 2 * quarter, entries, whole, "analysis_b")
    return whole[:, None]


def solution(mesh):
    in_specs = (
        P("mem", "reg", None, None),
        P("mem", "reg", None, None),
        P("reg", None, None),
        P("reg", None, None),
        P("reg", "mem"),
        P("reg", "mem", None),
    )
    out_specs = P("mem", "reg", None, None)
    return jax.shard_map(body, mesh=mesh, in_specs=in_specs, out_specs=out_specs, check_vma=False)
```

```python
import functools

import jax
import jax.numpy as jnp
from jax import lax
from jax.experimental import pallas as pl
from jax.experimental.pallas import tpu as pltpu
from jax.sharding import PartitionSpec as P

INNOV_ROWS = 16
SLOT_CHUNK = 256
MEMBER_TILE = 32
POOL_TILE = 256
TRANSFORM_CHUNK = 256
ANALYSIS_TILE = 256
MIB = 1024 * 1024


def pool_kernel(obs_ref, innov_ref, out_ref):
    members = obs_ref.shape[0]
    out_ref[:, :members, :] = jnp.swapaxes(obs_ref[...], 0, 1)
    shape = (out_ref.shape[0], INNOV_ROWS, out_ref.shape[2])
    out_ref[:, members:, :] = jnp.broadcast_to(innov_ref[...][:, None, :], shape)


def pool_rows(obs, innov):
    members, blocks, depth = obs.shape
    rows = members + INNOV_ROWS
    return pl.pallas_call(
        pool_kernel,
        grid=(depth // POOL_TILE,),
        in_specs=[
            pl.BlockSpec((members, blocks, POOL_TILE), lambda i: (0, 0, i)),
            pl.BlockSpec((blocks, POOL_TILE), lambda i: (0, i)),
        ],
        out_specs=pl.BlockSpec((blocks, rows, POOL_TILE), lambda i: (0, 0, i)),
        out_shape=jax.ShapeDtypeStruct((blocks, rows, depth), obs.dtype),
        compiler_params=pltpu.CompilerParams(vmem_limit_bytes=60 * MIB),
        cost_estimate=pl.CostEstimate(
            flops=0, bytes_accessed=4 * rows * blocks * depth, transcendentals=0
        ),
        name="pool_rows",
    )(obs, innov)


def gather_kernel(first, place_ref, own_ref, up_ref, down_ref, idx_ref, out_ref, *inn_refs):
    block = (pl.program_id(0) + first) ^ place_ref[0]
    blocks, rows, depth = own_ref.shape
    members = out_ref.shape[1]
    slots = out_ref.shape[2]
    if not inn_refs:
        rows = members
    west = jnp.maximum(block - 1, 0)
    east = jnp.minimum(block + 1, blocks - 1)
    sources = (
        (own_ref, block, None),
        (up_ref, block, None),
        (down_ref, block, None),
        (own_ref, west, block > 0),
        (own_ref, east, block < blocks - 1),
    )
    columns = lax.broadcasted_iota(jnp.int32, (depth, SLOT_CHUNK), 0)

    @pl.loop(0, slots // SLOT_CHUNK)
    def _(chunk):
        where = pl.ds(pl.multiple_of(chunk * SLOT_CHUNK, SLOT_CHUNK), SLOT_CHUNK)
        picks = idx_ref[pl.ds(block, 1), where]
        acc = jnp.zeros((rows, SLOT_CHUNK), jnp.float32)
        for number, (ref, at, live) in enumerate(sources):
            local = picks - number * depth
            if live is not None:
                local = jnp.where(live, local, -1)
            one_hot = jnp.where(columns == local, 1.0, 0.0).astype(jnp.bfloat16)
            acc += jnp.dot(ref[at, :rows], one_hot, preferred_element_type=jnp.float32)
        out_ref[0, :, where] = acc[:members].astype(jnp.bfloat16)
        for inn_ref in inn_refs:

            @pl.when(pl.program_id(0) == 0)
            def _():
                inn_ref[:, where] = acc[members:].astype(jnp.bfloat16)


def gather_chosen(place, own, up, down, picks, first, count, name):
    blocks, rows, depth = own.shape
    members = rows - INNOV_ROWS
    slots = picks.shape[1]
    vmem = pl.BlockSpec(memory_space=pltpu.VMEM)
    out_specs = [pl.BlockSpec((1, members, slots), lambda k: (k, 0, 0))]
    out_shape = [jax.ShapeDtypeStruct((count, members, slots), jnp.bfloat16)]
    if first == 0:
        out_specs.append(pl.BlockSpec((INNOV_ROWS, slots), lambda k: (0, 0)))
        out_shape.append(jax.ShapeDtypeStruct((INNOV_ROWS, slots), jnp.bfloat16))
    return pl.pallas_call(
        functools.partial(gather_kernel, first),
        grid=(count,),
        in_specs=[pl.BlockSpec(memory_space=pltpu.SMEM)] + [vmem] * 4,
        out_specs=out_specs,
        out_shape=out_shape,
        compiler_params=pltpu.CompilerParams(vmem_limit_bytes=40 * MIB),
        cost_estimate=pl.CostEstimate(
            flops=0,
            bytes_accessed=rows * slots,
            transcendentals=0,
        ),
        name=name,
    )(place, own, up, down, picks)


def to_blocks_kernel(in_ref, out_ref):
    out_ref[...] = jnp.swapaxes(in_ref[...], 0, 1)


def to_blocks(state, start, width, name):
    members, blocks, _ = state.shape
    return pl.pallas_call(
        to_blocks_kernel,
        grid=(members // MEMBER_TILE,),
        in_specs=[
            pl.BlockSpec((MEMBER_TILE, blocks, pl.Element(width)), lambda i: (i, 0, start))
            if start % width
            else pl.BlockSpec((MEMBER_TILE, blocks, width), lambda i: (i, 0, start // width))
        ],
        out_specs=pl.BlockSpec((blocks, MEMBER_TILE, width), lambda i: (0, i, 0)),
        out_shape=jax.ShapeDtypeStruct((blocks, members, width), state.dtype),
        compiler_params=pltpu.CompilerParams(vmem_limit_bytes=60 * MIB),
        cost_estimate=pl.CostEstimate(
            flops=0, bytes_accessed=4 * members * blocks * width, transcendentals=0
        ),
        name=name,
    )(state)


def to_members_kernel(part_ref, *refs):
    refs[-1][...] = jnp.swapaxes(part_ref[...], 0, 1)


def pairs_to_members_kernel(place_ref, *refs):
    *part_refs, out_ref, stage = refs
    for number, ref in enumerate(part_refs):
        stage[place_ref[0] ^ number] = ref[...]
    out_ref[...] = jnp.swapaxes(stage[...], 0, 1)


def to_members(part, start, entries, whole, name):
    blocks, members, width = part.shape
    return pl.pallas_call(
        to_members_kernel,
        grid=(members // MEMBER_TILE,),
        in_specs=[
            pl.BlockSpec((blocks, MEMBER_TILE, width), lambda i: (0, i, 0)),
            pl.BlockSpec(memory_space=pl.ANY),
        ],
        out_specs=pl.BlockSpec((MEMBER_TILE, blocks, width), lambda i: (i, 0, start // width)),
        out_shape=jax.ShapeDtypeStruct((members, blocks, entries), part.dtype),
        input_output_aliases={1: 0},
        compiler_params=pltpu.CompilerParams(vmem_limit_bytes=32 * MIB),
        cost_estimate=pl.CostEstimate(
            flops=0, bytes_accessed=4 * members * blocks * width, transcendentals=0
        ),
        name=name,
    )(part, whole)


def pairs_to_members(place, parts, start, entries, name):
    blocks = len(parts)
    members, width = parts[0].shape
    return pl.pallas_call(
        pairs_to_members_kernel,
        grid=(members // MEMBER_TILE,),
        in_specs=[pl.BlockSpec(memory_space=pltpu.SMEM)]
        + [pl.BlockSpec((MEMBER_TILE, width), lambda i: (i, 0))] * blocks,
        out_specs=pl.BlockSpec((MEMBER_TILE, blocks, width), lambda i: (i, 0, start // width)),
        out_shape=jax.ShapeDtypeStruct((members, blocks, entries), parts[0].dtype),
        scratch_shapes=[pltpu.VMEM((blocks, MEMBER_TILE, width), parts[0].dtype)],
        compiler_params=pltpu.CompilerParams(vmem_limit_bytes=32 * MIB),
        cost_estimate=pl.CostEstimate(
            flops=0, bytes_accessed=4 * members * blocks * width, transcendentals=0
        ),
        name=name,
    )(place, *parts)


def transform_kernel(place_ref, tally_ref, weight_ref, innov_ref, *refs):
    *part_refs, out_ref, obs_ref = refs[:-7]
    weighted, precision, root, step, root_next, step_next, inverse = refs[-7:]
    count_k, slots = obs_ref.shape
    members = count_k // len(part_refs)
    for number, ref in enumerate(part_refs):
        at = pl.multiple_of((place_ref[0] ^ number) * members, members)
        obs_ref[pl.ds(at, members), :] = ref[...]
    spare = count_k - 1.0
    chunks = count_k // TRANSFORM_CHUNK
    live = lax.broadcasted_iota(jnp.int32, (1, slots), 1) < tally_ref[0, 0]
    obs_weight = jnp.where(live, weight_ref[...], 0.0)

    def span(chunk):
        return pl.ds(pl.multiple_of(chunk * TRANSFORM_CHUNK, TRANSFORM_CHUNK), TRANSFORM_CHUNK)

    def on_diagonal(chunk, value):
        rows = lax.broadcasted_iota(jnp.int32, (count_k, TRANSFORM_CHUNK), 0)
        columns = lax.broadcasted_iota(jnp.int32, (count_k, TRANSFORM_CHUNK), 1)
        return jnp.where(rows == columns + chunk * TRANSFORM_CHUNK, value, 0.0)

    def matmul(left, right):
        return jnp.dot(left, right, preferred_element_type=jnp.float32)

    def by_rows(left, right):
        return lax.dot_general(
            left, right, (((1,), (1,)), ((), ())), preferred_element_type=jnp.float32
        )

    def precise(row, matrix):
        high = row.astype(jnp.bfloat16)
        rest = row - high.astype(jnp.float32)
        middle = rest.astype(jnp.bfloat16)
        low = (rest - middle.astype(jnp.float32)).astype(jnp.bfloat16)
        return (matmul(low, matrix) + matmul(middle, matrix)) + matmul(high, matrix)

    def weigh(chunk, trace):
        at = span(chunk)
        scaled = (obs_ref[at, :].astype(jnp.float32) * obs_weight).astype(jnp.bfloat16)
        weighted[at, :] = scaled
        product = by_rows(obs_ref[...], scaled)
        precision[:, at] = product
        return trace + jnp.sum(on_diagonal(chunk, product))

    trace = lax.fori_loop(0, chunks, weigh, jnp.float32(0.0))
    trace_mean = trace / count_k + spare
    scale = 1.0 / trace_mean
    gain = by_rows(innov_ref[...], weighted[...])

    @pl.loop(0, chunks)
    def _(chunk):
        at = span(chunk)
        first = ((precision[:, at] + on_diagonal(chunk, spare)) * scale).astype(jnp.bfloat16)
        root[:, at] = first
        step[:, at] = (on_diagonal(chunk, 1.5) - 0.5 * first.astype(jnp.float32)).astype(jnp.bfloat16)

    @pl.loop(0, chunks)
    def _(chunk):
        at = span(chunk)
        root_next[:, at] = matmul(step[...], root[:, at]).astype(jnp.bfloat16)

    @pl.loop(0, chunks)
    def _(chunk):
        at = span(chunk)
        product = matmul(root_next[...], step[:, at])
        step_next[:, at] = (on_diagonal(chunk, 1.5) - 0.5 * product).astype(jnp.bfloat16)

    @pl.loop(0, chunks)
    def _(chunk):
        at = span(chunk)
        inverse[:, at] = matmul(step[...], step_next[:, at]).astype(jnp.bfloat16)

    inner = precise(gain, inverse[...])
    mean_weight = precise(inner, inverse[...])[:1] * scale
    spread_factor = jnp.sqrt(jnp.full((1, slots), spare * scale, jnp.float32))
    out_ref[...] = (
        spread_factor[:, :count_k] * inverse[...].astype(jnp.float32) + mean_weight
    ).astype(jnp.bfloat16)


def ensemble_transform(place, tally, weight, innov, parts):
    members, slots = parts[0].shape
    count_k = members * len(parts)
    vmem = pl.BlockSpec(memory_space=pltpu.VMEM)
    square = pltpu.VMEM((count_k, count_k), jnp.bfloat16)
    return pl.pallas_call(
        transform_kernel,
        in_specs=[pl.BlockSpec(memory_space=pltpu.SMEM)] * 2 + [vmem] * (2 + len(parts)),
        out_specs=vmem,
        out_shape=jax.ShapeDtypeStruct((count_k, count_k), jnp.bfloat16),
        scratch_shapes=[
            pltpu.VMEM((count_k, slots), jnp.bfloat16),
            pltpu.VMEM((count_k, slots), jnp.bfloat16),
            pltpu.VMEM((count_k, count_k), jnp.float32),
            square, square, square, square, square,
        ],
        compiler_params=pltpu.CompilerParams(vmem_limit_bytes=40 * MIB),
        cost_estimate=pl.CostEstimate(
            flops=0,
            bytes_accessed=count_k * slots,
            transcendentals=0,
        ),
        name="transform",
    )(place, tally, weight, innov, *parts)


def analysis_kernel(in_pairs, place_ref, transform_ref, state_ref, out_ref, stage):
    blocks, members, width = out_ref.shape
    state = state_ref[...].astype(jnp.float32)
    state_mean = jnp.sum(state, axis=0, keepdims=True) * (1.0 / state.shape[0])
    perturb = (state - state_mean).astype(jnp.bfloat16)
    increment = jnp.dot(transform_ref[...], perturb, preferred_element_type=jnp.float32)
    result = (state_mean + increment).astype(jnp.bfloat16).reshape(out_ref.shape)
    if in_pairs:
        stage[...] = result
        for number in range(blocks):
            out_ref[number] = stage[place_ref[0] ^ number]
    else:
        out_ref[...] = result


def analysed(place, transform, part, in_pairs, name):
    blocks, members, width = part.shape
    count_k = blocks * members
    return pl.pallas_call(
        functools.partial(analysis_kernel, in_pairs),
        grid=(width // ANALYSIS_TILE,),
        in_specs=[
            pl.BlockSpec(memory_space=pltpu.SMEM),
            pl.BlockSpec(memory_space=pltpu.VMEM),
            pl.BlockSpec((count_k, ANALYSIS_TILE), lambda i: (0, i)),
        ],
        out_specs=pl.BlockSpec((blocks, members, ANALYSIS_TILE), lambda i: (0, 0, i)),
        out_shape=jax.ShapeDtypeStruct(part.shape, jnp.bfloat16),
        scratch_shapes=[pltpu.VMEM((blocks, members, ANALYSIS_TILE), jnp.bfloat16)],
        compiler_params=pltpu.CompilerParams(vmem_limit_bytes=32 * MIB),
        cost_estimate=pl.CostEstimate(
            flops=2 * count_k * count_k * width,
            bytes_accessed=2 * count_k * (2 * width + count_k),
            transcendentals=0,
        ),
        name=name,
    )(place, transform, part.reshape(count_k, width))


def body(
    prior_members_field,
    measure_space_deviations,
    measured_minus_predicted,
    measure_pool_indices,
    active_measure_tally,
    tapered_error_weight,
):
    place = lax.axis_index("mem").astype(jnp.int32).reshape(1)
    strips = lax.axis_size("reg")
    devices = lax.axis_size("mem")
    entries = prior_members_field.shape[3]
    to_next = [(i, i + 1) for i in range(strips - 1)]
    to_last = [(i + 1, i) for i in range(strips - 1)]

    def exchange(x):
        return lax.all_to_all(x, "mem", split_axis=0, concat_axis=0, tiled=True)

    def swap(x, number):
        return lax.ppermute(x, "mem", [(i, i ^ number) for i in range(devices)])

    half = devices // 2
    quarter = entries // 4
    state = prior_members_field[:, 0]
    state_a = to_blocks(state, 0, 2 * quarter, "state_a")
    devs, state_a = lax.optimization_barrier((measure_space_deviations[:, 0], state_a))
    state_a = exchange(state_a)
    pool = pool_rows(devs, measured_minus_predicted[0])
    up = lax.ppermute(pool, "reg", to_next)
    down = lax.ppermute(pool, "reg", to_last)
    picks = measure_pool_indices[0]
    far = gather_chosen(place, pool, up, down, picks, half, half, "gather_far")[0]
    far = [swap(far[k], k + half) for k in range(half)]
    near, innov = gather_chosen(place, pool, up, down, picks, 0, half, "gather_near")
    near = [near[0]] + [swap(near[k], k) for k in range(1, half)]
    state_b = to_blocks(state, 2 * quarter, 2 * quarter, "state_b")
    state_b, state_a, near, far = lax.optimization_barrier((state_b, state_a, near, far))
    state_b = exchange(state_b)
    transform = ensemble_transform(
        place, active_measure_tally, tapered_error_weight[0], innov, near + far
    )
    done_a = analysed(place, transform, state_a, True, "analysed_a")
    done_a, state_b = lax.optimization_barrier((done_a, state_b))
    done_a = [done_a[0]] + [swap(done_a[k], k) for k in range(1, devices)]
    done_b = exchange(analysed(place, transform, state_b, False, "analysed_b"))
    whole = pairs_to_members(place, done_a, 0, entries, "analysis_a")
    whole = to_members(done_b, 2 * quarter, entries, whole, "analysis_b")
    return whole[:, None]


def solution(mesh):
    in_specs = (
        P("mem", "reg", None, None),
        P("mem", "reg", None, None),
        P("reg", None, None),
        P("reg", None, None),
        P("reg", "mem"),
        P("reg", "mem", None),
    )
    out_specs = P("mem", "reg", None, None)
    return jax.shard_map(body, mesh=mesh, in_specs=in_specs, out_specs=out_specs, check_vma=False)
```

```python
import functools

import jax
import jax.numpy as jnp
from jax import lax
from jax.experimental import pallas as pl
from jax.experimental.pallas import tpu as pltpu
from jax.sharding import PartitionSpec as P

INNOV_ROWS = 16
SLOT_CHUNK = 256
MEMBER_TILE = 32
POOL_TILE = 256
TRANSFORM_CHUNK = 256
ANALYSIS_TILE = 256
MIB = 1024 * 1024


def pool_kernel(obs_ref, innov_ref, out_ref):
    members = obs_ref.shape[0]
    out_ref[:, :members, :] = jnp.swapaxes(obs_ref[...], 0, 1)
    shape = (out_ref.shape[0], INNOV_ROWS, out_ref.shape[2])
    out_ref[:, members:, :] = jnp.broadcast_to(innov_ref[...][:, None, :], shape)


def pool_rows(obs, innov):
    members, blocks, depth = obs.shape
    rows = members + INNOV_ROWS
    return pl.pallas_call(
        pool_kernel,
        grid=(depth // POOL_TILE,),
        in_specs=[
            pl.BlockSpec((members, blocks, POOL_TILE), lambda i: (0, 0, i)),
            pl.BlockSpec((blocks, POOL_TILE), lambda i: (0, i)),
        ],
        out_specs=pl.BlockSpec((blocks, rows, POOL_TILE), lambda i: (0, 0, i)),
        out_shape=jax.ShapeDtypeStruct((blocks, rows, depth), obs.dtype),
        compiler_params=pltpu.CompilerParams(vmem_limit_bytes=60 * MIB),
        cost_estimate=pl.CostEstimate(
            flops=0, bytes_accessed=4 * rows * blocks * depth, transcendentals=0
        ),
        name="pool_rows",
    )(obs, innov)


def gather_kernel(first, place_ref, own_ref, up_ref, down_ref, idx_ref, out_ref, *inn_refs):
    block = (pl.program_id(0) + first) ^ place_ref[0]
    blocks, rows, depth = own_ref.shape
    members = out_ref.shape[1]
    slots = out_ref.shape[2]
    if not inn_refs:
        rows = members
    west = jnp.maximum(block - 1, 0)
    east = jnp.minimum(block + 1, blocks - 1)
    sources = (
        (own_ref, block, None),
        (up_ref, block, None),
        (down_ref, block, None),
        (own_ref, west, block > 0),
        (own_ref, east, block < blocks - 1),
    )
    columns = lax.broadcasted_iota(jnp.int32, (depth, SLOT_CHUNK), 0)

    @pl.loop(0, slots // SLOT_CHUNK)
    def _(chunk):
        where = pl.ds(pl.multiple_of(chunk * SLOT_CHUNK, SLOT_CHUNK), SLOT_CHUNK)
        picks = idx_ref[pl.ds(block, 1), where]
        acc = jnp.zeros((rows, SLOT_CHUNK), jnp.float32)
        for number, (ref, at, live) in enumerate(sources):
            local = picks - number * depth
            if live is not None:
                local = jnp.where(live, local, -1)
            one_hot = jnp.where(columns == local, 1.0, 0.0).astype(jnp.bfloat16)
            acc += jnp.dot(ref[at, :rows], one_hot, preferred_element_type=jnp.float32)
        out_ref[0, :, where] = acc[:members].astype(jnp.bfloat16)
        for inn_ref in inn_refs:

            @pl.when(pl.program_id(0) == 0)
            def _():
                inn_ref[:, where] = acc[members:].astype(jnp.bfloat16)


def gather_chosen(place, own, up, down, picks, first, count, name):
    blocks, rows, depth = own.shape
    members = rows - INNOV_ROWS
    slots = picks.shape[1]
    vmem = pl.BlockSpec(memory_space=pltpu.VMEM)
    out_specs = [pl.BlockSpec((1, members, slots), lambda k: (k, 0, 0))]
    out_shape = [jax.ShapeDtypeStruct((count, members, slots), jnp.bfloat16)]
    if first == 0:
        out_specs.append(pl.BlockSpec((INNOV_ROWS, slots), lambda k: (0, 0)))
        out_shape.append(jax.ShapeDtypeStruct((INNOV_ROWS, slots), jnp.bfloat16))
    return pl.pallas_call(
        functools.partial(gather_kernel, first),
        grid=(count,),
        in_specs=[pl.BlockSpec(memory_space=pltpu.SMEM)] + [vmem] * 4,
        out_specs=out_specs,
        out_shape=out_shape,
        compiler_params=pltpu.CompilerParams(vmem_limit_bytes=40 * MIB),
        cost_estimate=pl.CostEstimate(
            flops=0,
            bytes_accessed=rows * slots,
            transcendentals=0,
        ),
        name=name,
    )(place, own, up, down, picks)


def to_blocks_kernel(in_ref, out_ref):
    out_ref[...] = jnp.swapaxes(in_ref[...], 0, 1)


def to_blocks(state, start, width, name):
    members, blocks, _ = state.shape
    return pl.pallas_call(
        to_blocks_kernel,
        grid=(members // MEMBER_TILE,),
        in_specs=[
            pl.BlockSpec((MEMBER_TILE, blocks, pl.Element(width)), lambda i: (i, 0, start))
            if start % width
            else pl.BlockSpec((MEMBER_TILE, blocks, width), lambda i: (i, 0, start // width))
        ],
        out_specs=pl.BlockSpec((blocks, MEMBER_TILE, width), lambda i: (0, i, 0)),
        out_shape=jax.ShapeDtypeStruct((blocks, members, width), state.dtype),
        compiler_params=pltpu.CompilerParams(vmem_limit_bytes=60 * MIB),
        cost_estimate=pl.CostEstimate(
            flops=0, bytes_accessed=4 * members * blocks * width, transcendentals=0
        ),
        name=name,
    )(state)


def to_members_kernel(part_ref, *refs):
    refs[-1][...] = jnp.swapaxes(part_ref[...], 0, 1)


def pairs_to_members_kernel(place_ref, *refs):
    *part_refs, out_ref, stage = refs
    for number, ref in enumerate(part_refs):
        stage[place_ref[0] ^ number] = ref[...]
    out_ref[...] = jnp.swapaxes(stage[...], 0, 1)


def to_members(part, start, entries, whole, name):
    blocks, members, width = part.shape
    return pl.pallas_call(
        to_members_kernel,
        grid=(members // MEMBER_TILE,),
        in_specs=[
            pl.BlockSpec((blocks, MEMBER_TILE, width), lambda i: (0, i, 0)),
            pl.BlockSpec(memory_space=pl.ANY),
        ],
        out_specs=pl.BlockSpec((MEMBER_TILE, blocks, width), lambda i: (i, 0, start // width)),
        out_shape=jax.ShapeDtypeStruct((members, blocks, entries), part.dtype),
        input_output_aliases={1: 0},
        compiler_params=pltpu.CompilerParams(vmem_limit_bytes=32 * MIB),
        cost_estimate=pl.CostEstimate(
            flops=0, bytes_accessed=4 * members * blocks * width, transcendentals=0
        ),
        name=name,
    )(part, whole)


def pairs_to_members(place, parts, start, entries, name):
    blocks = len(parts)
    members, width = parts[0].shape
    return pl.pallas_call(
        pairs_to_members_kernel,
        grid=(members // MEMBER_TILE,),
        in_specs=[pl.BlockSpec(memory_space=pltpu.SMEM)]
        + [pl.BlockSpec((MEMBER_TILE, width), lambda i: (i, 0))] * blocks,
        out_specs=pl.BlockSpec((MEMBER_TILE, blocks, width), lambda i: (i, 0, start // width)),
        out_shape=jax.ShapeDtypeStruct((members, blocks, entries), parts[0].dtype),
        scratch_shapes=[pltpu.VMEM((blocks, MEMBER_TILE, width), parts[0].dtype)],
        compiler_params=pltpu.CompilerParams(vmem_limit_bytes=32 * MIB),
        cost_estimate=pl.CostEstimate(
            flops=0, bytes_accessed=4 * members * blocks * width, transcendentals=0
        ),
        name=name,
    )(place, *parts)


def transform_kernel(place_ref, tally_ref, weight_ref, innov_ref, *refs):
    *part_refs, out_ref, obs_ref = refs[:-8]
    weighted, precision, root, step, root_next, step_next, inverse, arrived = refs[-8:]
    count_k, slots = obs_ref.shape
    members = count_k // len(part_refs)
    copies = []
    for number, ref in enumerate(part_refs):
        at = pl.multiple_of((place_ref[0] ^ number) * members, members)
        copies.append(
            pltpu.make_async_copy(ref, obs_ref.at[pl.ds(at, members)], arrived.at[number])
        )
    for copy in copies:
        copy.start()
    for copy in copies:
        copy.wait()
    spare = count_k - 1.0
    chunks = count_k // TRANSFORM_CHUNK
    live = lax.broadcasted_iota(jnp.int32, (1, slots), 1) < tally_ref[0, 0]
    obs_weight = jnp.where(live, weight_ref[...], 0.0)

    def span(chunk):
        return pl.ds(pl.multiple_of(chunk * TRANSFORM_CHUNK, TRANSFORM_CHUNK), TRANSFORM_CHUNK)

    def on_diagonal(chunk, value):
        rows = lax.broadcasted_iota(jnp.int32, (count_k, TRANSFORM_CHUNK), 0)
        columns = lax.broadcasted_iota(jnp.int32, (count_k, TRANSFORM_CHUNK), 1)
        return jnp.where(rows == columns + chunk * TRANSFORM_CHUNK, value, 0.0)

    def matmul(left, right):
        return jnp.dot(left, right, preferred_element_type=jnp.float32)

    def by_rows(left, right):
        return lax.dot_general(
            left, right, (((1,), (1,)), ((), ())), preferred_element_type=jnp.float32
        )

    def precise(row, matrix):
        high = row.astype(jnp.bfloat16)
        rest = row - high.astype(jnp.float32)
        middle = rest.astype(jnp.bfloat16)
        low = (rest - middle.astype(jnp.float32)).astype(jnp.bfloat16)
        return (matmul(low, matrix) + matmul(middle, matrix)) + matmul(high, matrix)

    def weigh(chunk, trace):
        at = span(chunk)
        scaled = (obs_ref[at, :].astype(jnp.float32) * obs_weight).astype(jnp.bfloat16)
        weighted[at, :] = scaled
        product = by_rows(obs_ref[...], scaled)
        precision[:, at] = product
        return trace + jnp.sum(on_diagonal(chunk, product))

    trace = lax.fori_loop(0, chunks, weigh, jnp.float32(0.0))
    trace_mean = trace / count_k + spare
    scale = 1.0 / trace_mean
    gain = by_rows(innov_ref[...], weighted[...])

    @pl.loop(0, chunks)
    def _(chunk):
        at = span(chunk)
        first = ((precision[:, at] + on_diagonal(chunk, spare)) * scale).astype(jnp.bfloat16)
        root[:, at] = first
        step[:, at] = (on_diagonal(chunk, 1.5) - 0.5 * first.astype(jnp.float32)).astype(jnp.bfloat16)

    @pl.loop(0, chunks)
    def _(chunk):
        at = span(chunk)
        root_next[:, at] = matmul(step[...], root[:, at]).astype(jnp.bfloat16)

    @pl.loop(0, chunks)
    def _(chunk):
        at = span(chunk)
        product = matmul(root_next[...], step[:, at])
        step_next[:, at] = (on_diagonal(chunk, 1.5) - 0.5 * product).astype(jnp.bfloat16)

    @pl.loop(0, chunks)
    def _(chunk):
        at = span(chunk)
        inverse[:, at] = matmul(step[...], step_next[:, at]).astype(jnp.bfloat16)

    inner = precise(gain, inverse[...])
    mean_weight = precise(inner, inverse[...])[:1] * scale
    spread_factor = jnp.sqrt(jnp.full((1, slots), spare * scale, jnp.float32))
    out_ref[...] = (
        spread_factor[:, :count_k] * inverse[...].astype(jnp.float32) + mean_weight
    ).astype(jnp.bfloat16)


def ensemble_transform(place, tally, weight, innov, parts):
    members, slots = parts[0].shape
    count_k = members * len(parts)
    vmem = pl.BlockSpec(memory_space=pltpu.VMEM)
    square = pltpu.VMEM((count_k, count_k), jnp.bfloat16)
    return pl.pallas_call(
        transform_kernel,
        in_specs=[pl.BlockSpec(memory_space=pltpu.SMEM)] * 2
        + [vmem] * 2
        + [pl.BlockSpec(memory_space=pl.ANY)] * len(parts),
        out_specs=vmem,
        out_shape=jax.ShapeDtypeStruct((count_k, count_k), jnp.bfloat16),
        scratch_shapes=[
            pltpu.VMEM((count_k, slots), jnp.bfloat16),
            pltpu.VMEM((count_k, slots), jnp.bfloat16),
            pltpu.VMEM((count_k, count_k), jnp.float32),
            square, square, square, square, square,
            pltpu.SemaphoreType.DMA((len(parts),)),
        ],
        compiler_params=pltpu.CompilerParams(vmem_limit_bytes=40 * MIB),
        cost_estimate=pl.CostEstimate(
            flops=0,
            bytes_accessed=count_k * slots,
            transcendentals=0,
        ),
        name="transform",
    )(place, tally, weight, innov, *parts)


def analysis_kernel(in_pairs, place_ref, transform_ref, state_ref, out_ref, stage):
    blocks, members, width = out_ref.shape
    state = state_ref[...].astype(jnp.float32)
    state_mean = jnp.sum(state, axis=0, keepdims=True) * (1.0 / state.shape[0])
    perturb = (state - state_mean).astype(jnp.bfloat16)
    increment = jnp.dot(transform_ref[...], perturb, preferred_element_type=jnp.float32)
    result = (state_mean + increment).astype(jnp.bfloat16).reshape(out_ref.shape)
    if in_pairs:
        stage[...] = result
        for number in range(blocks):
            out_ref[number] = stage[place_ref[0] ^ number]
    else:
        out_ref[...] = result


def analysed(place, transform, part, in_pairs, name):
    blocks, members, width = part.shape
    count_k = blocks * members
    return pl.pallas_call(
        functools.partial(analysis_kernel, in_pairs),
        grid=(width // ANALYSIS_TILE,),
        in_specs=[
            pl.BlockSpec(memory_space=pltpu.SMEM),
            pl.BlockSpec(memory_space=pltpu.VMEM),
            pl.BlockSpec((count_k, ANALYSIS_TILE), lambda i: (0, i)),
        ],
        out_specs=pl.BlockSpec((blocks, members, ANALYSIS_TILE), lambda i: (0, 0, i)),
        out_shape=jax.ShapeDtypeStruct(part.shape, jnp.bfloat16),
        scratch_shapes=[pltpu.VMEM((blocks, members, ANALYSIS_TILE), jnp.bfloat16)],
        compiler_params=pltpu.CompilerParams(vmem_limit_bytes=32 * MIB),
        cost_estimate=pl.CostEstimate(
            flops=0,
            bytes_accessed=count_k * width,
            transcendentals=0,
        ),
        name=name,
    )(place, transform, part.reshape(count_k, width))


def body(
    prior_members_field,
    measure_space_deviations,
    measured_minus_predicted,
    measure_pool_indices,
    active_measure_tally,
    tapered_error_weight,
):
    place = lax.axis_index("mem").astype(jnp.int32).reshape(1)
    strips = lax.axis_size("reg")
    devices = lax.axis_size("mem")
    entries = prior_members_field.shape[3]
    to_next = [(i, i + 1) for i in range(strips - 1)]
    to_last = [(i + 1, i) for i in range(strips - 1)]

    def exchange(x):
        return lax.all_to_all(x, "mem", split_axis=0, concat_axis=0, tiled=True)

    def swap(x, number):
        return lax.ppermute(x, "mem", [(i, i ^ number) for i in range(devices)])

    half = devices // 2
    quarter = entries // 4
    state = prior_members_field[:, 0]
    state_a = to_blocks(state, 0, 2 * quarter, "state_a")
    devs, state_a = lax.optimization_barrier((measure_space_deviations[:, 0], state_a))
    state_a = exchange(state_a)
    pool = pool_rows(devs, measured_minus_predicted[0])
    up = lax.ppermute(pool, "reg", to_next)
    down = lax.ppermute(pool, "reg", to_last)
    picks = measure_pool_indices[0]
    far = gather_chosen(place, pool, up, down, picks, half, half, "gather_far")[0]
    pool, far = lax.optimization_barrier((pool, far))
    far = [swap(far[k], k + half) for k in range(half)]
    near, innov = gather_chosen(place, pool, up, down, picks, 0, half, "gather_near")
    near = [near[0]] + [swap(near[k], k) for k in range(1, half)]
    state_b = to_blocks(state, 2 * quarter, 2 * quarter, "state_b")
    state_b, state_a, near, far = lax.optimization_barrier((state_b, state_a, near, far))
    state_b = exchange(state_b)
    transform = ensemble_transform(
        place, active_measure_tally, tapered_error_weight[0], innov, near + far
    )
    done_a = analysed(place, transform, state_a, True, "analysed_a")
    transform, done_a = lax.optimization_barrier((transform, done_a))
    done_a = [done_a[0]] + [swap(done_a[k], k) for k in range(1, devices)]
    done_b = analysed(place, transform, state_b, False, "analysed_b")
    done_b, *done_a[half : half + 2] = lax.optimization_barrier(
        (done_b, *done_a[half : half + 2])
    )
    done_b = exchange(done_b)
    whole = pairs_to_members(place, done_a, 0, entries, "analysis_a")
    whole = to_members(done_b, 2 * quarter, entries, whole, "analysis_b")
    return whole[:, None]


def solution(mesh):
    in_specs = (
        P("mem", "reg", None, None),
        P("mem", "reg", None, None),
        P("reg", None, None),
        P("reg", None, None),
        P("reg", "mem"),
        P("reg", "mem", None),
    )
    out_specs = P("mem", "reg", None, None)
    return jax.shard_map(body, mesh=mesh, in_specs=in_specs, out_specs=out_specs, check_vma=False)
```

```python
import functools

import jax
import jax.numpy as jnp
from jax import lax
from jax.experimental import pallas as pl
from jax.experimental.pallas import tpu as pltpu
from jax.sharding import PartitionSpec as P

INNOV_ROWS = 16
SLOT_CHUNK = 256
MEMBER_TILE = 32
TRANSFORM_CHUNK = 256
ANALYSIS_TILE = 256
MIB = 1024 * 1024


def fetch_tiles(source_ref, start, stage, arrived, use):
    width = stage.shape[2]
    tiles = []
    for number in range(stage.shape[0] // MEMBER_TILE):
        rows = pl.ds(number * MEMBER_TILE, MEMBER_TILE)
        copy = pltpu.make_async_copy(
            source_ref.at[rows, :, pl.ds(start, width)], stage.at[rows], arrived.at[number]
        )
        copy.start()
        tiles.append((copy, rows))
    for copy, rows in tiles:
        copy.wait()
        use(rows)


def to_blocks_kernel(start, state_ref, out_ref, stage, arrived):
    def use(rows):
        out_ref[:, rows, :] = jnp.swapaxes(stage[rows], 0, 1)

    fetch_tiles(state_ref, start, stage, arrived, use)


def to_blocks(state, start, width, name):
    members, blocks, _ = state.shape
    return pl.pallas_call(
        functools.partial(to_blocks_kernel, start),
        in_specs=[pl.BlockSpec(memory_space=pltpu.HBM)],
        out_specs=pl.BlockSpec(memory_space=pltpu.VMEM),
        out_shape=jax.ShapeDtypeStruct((blocks, members, width), state.dtype),
        scratch_shapes=[
            pltpu.VMEM((members, blocks, width), state.dtype),
            pltpu.SemaphoreType.DMA((members // MEMBER_TILE,)),
        ],
        compiler_params=pltpu.CompilerParams(vmem_limit_bytes=60 * MIB),
        cost_estimate=pl.CostEstimate(
            flops=0, bytes_accessed=4 * members * blocks * width, transcendentals=0
        ),
        name=name,
    )(state)


def pool_kernel(obs_ref, innov_ref, out_ref, stage, arrived):
    members = obs_ref.shape[0]

    def use(rows):
        out_ref[:, rows, :] = jnp.swapaxes(stage[rows], 0, 1)

    shape = (out_ref.shape[0], INNOV_ROWS, out_ref.shape[2])
    out_ref[:, members:, :] = jnp.broadcast_to(innov_ref[...][:, None, :], shape)
    fetch_tiles(obs_ref, 0, stage, arrived, use)


def pool_rows(obs, innov):
    members, blocks, depth = obs.shape
    rows = members + INNOV_ROWS
    vmem = pl.BlockSpec(memory_space=pltpu.VMEM)
    return pl.pallas_call(
        pool_kernel,
        in_specs=[pl.BlockSpec(memory_space=pltpu.HBM), vmem],
        out_specs=vmem,
        out_shape=jax.ShapeDtypeStruct((blocks, rows, depth), obs.dtype),
        scratch_shapes=[
            pltpu.VMEM((members, blocks, depth), obs.dtype),
            pltpu.SemaphoreType.DMA((members // MEMBER_TILE,)),
        ],
        compiler_params=pltpu.CompilerParams(vmem_limit_bytes=60 * MIB),
        cost_estimate=pl.CostEstimate(
            flops=0, bytes_accessed=4 * rows * blocks * depth, transcendentals=0
        ),
        name="pool_rows",
    )(obs, innov)


def gather_kernel(first, place_ref, own_ref, up_ref, down_ref, idx_ref, out_ref, *inn_refs):
    block = (pl.program_id(0) + first) ^ place_ref[0]
    blocks, rows, depth = own_ref.shape
    members = out_ref.shape[1]
    slots = out_ref.shape[2]
    if not inn_refs:
        rows = members
    west = jnp.maximum(block - 1, 0)
    east = jnp.minimum(block + 1, blocks - 1)
    sources = (
        (own_ref, block, None),
        (up_ref, block, None),
        (down_ref, block, None),
        (own_ref, west, block > 0),
        (own_ref, east, block < blocks - 1),
    )
    columns = lax.broadcasted_iota(jnp.int32, (depth, SLOT_CHUNK), 0)

    @pl.loop(0, slots // SLOT_CHUNK)
    def _(chunk):
        where = pl.ds(pl.multiple_of(chunk * SLOT_CHUNK, SLOT_CHUNK), SLOT_CHUNK)
        picks = idx_ref[pl.ds(block, 1), where]
        acc = jnp.zeros((rows, SLOT_CHUNK), jnp.float32)
        for number, (ref, at, live) in enumerate(sources):
            local = picks - number * depth
            if live is not None:
                local = jnp.where(live, local, -1)
            one_hot = jnp.where(columns == local, 1.0, 0.0).astype(jnp.bfloat16)
            acc += jnp.dot(ref[at, :rows], one_hot, preferred_element_type=jnp.float32)
        out_ref[0, :, where] = acc[:members].astype(jnp.bfloat16)
        for inn_ref in inn_refs:

            @pl.when(pl.program_id(0) == 0)
            def _():
                inn_ref[:, where] = acc[members:].astype(jnp.bfloat16)


def gather_chosen(place, own, up, down, picks, first, count, name):
    blocks, rows, depth = own.shape
    members = rows - INNOV_ROWS
    slots = picks.shape[1]
    vmem = pl.BlockSpec(memory_space=pltpu.VMEM)
    out_specs = [pl.BlockSpec((1, members, slots), lambda k: (k, 0, 0))]
    out_shape = [jax.ShapeDtypeStruct((count, members, slots), jnp.bfloat16)]
    if first == 0:
        out_specs.append(pl.BlockSpec((INNOV_ROWS, slots), lambda k: (0, 0)))
        out_shape.append(jax.ShapeDtypeStruct((INNOV_ROWS, slots), jnp.bfloat16))
    return pl.pallas_call(
        functools.partial(gather_kernel, first),
        grid=(count,),
        in_specs=[pl.BlockSpec(memory_space=pltpu.SMEM)] + [vmem] * 4,
        out_specs=out_specs,
        out_shape=out_shape,
        compiler_params=pltpu.CompilerParams(vmem_limit_bytes=40 * MIB),
        cost_estimate=pl.CostEstimate(
            flops=0,
            bytes_accessed=rows * slots,
            transcendentals=0,
        ),
        name=name,
    )(place, own, up, down, picks)


def store_tiles(out_ref, start, stage, sent, make):
    width = stage.shape[2]
    copies = []
    for number in range(stage.shape[0] // MEMBER_TILE):
        rows = pl.ds(number * MEMBER_TILE, MEMBER_TILE)
        stage[rows] = make(rows)
        copy = pltpu.make_async_copy(
            stage.at[rows], out_ref.at[rows, :, pl.ds(start, width)], sent.at[number]
        )
        copy.start()
        copies.append(copy)
    for copy in copies:
        copy.wait()


def to_members_kernel(start, part_ref, whole_ref, out_ref, stage, sent):
    store_tiles(out_ref, start, stage, sent, lambda rows: jnp.swapaxes(part_ref[:, rows, :], 0, 1))


def pairs_to_members_kernel(start, place_ref, *refs):
    *part_refs, out_ref, turned, stage, sent = refs

    def make(rows):
        for number, ref in enumerate(part_refs):
            turned[place_ref[0] ^ number] = ref[rows]
        return jnp.swapaxes(turned[...], 0, 1)

    store_tiles(out_ref, start, stage, sent, make)


def to_members(part, start, whole, name):
    blocks, members, width = part.shape
    hbm = pl.BlockSpec(memory_space=pltpu.HBM)
    return pl.pallas_call(
        functools.partial(to_members_kernel, start),
        in_specs=[pl.BlockSpec(memory_space=pltpu.VMEM), hbm],
        out_specs=hbm,
        out_shape=jax.ShapeDtypeStruct(whole.shape, part.dtype),
        scratch_shapes=[
            pltpu.VMEM((members, blocks, width), part.dtype),
            pltpu.SemaphoreType.DMA((members // MEMBER_TILE,)),
        ],
        input_output_aliases={1: 0},
        compiler_params=pltpu.CompilerParams(vmem_limit_bytes=16 * MIB),
        cost_estimate=pl.CostEstimate(
            flops=0, bytes_accessed=4 * members * blocks * width, transcendentals=0
        ),
        name=name,
    )(part, whole)


def pairs_to_members(place, parts, start, entries, name):
    blocks = len(parts)
    members, width = parts[0].shape
    return pl.pallas_call(
        functools.partial(pairs_to_members_kernel, start),
        in_specs=[pl.BlockSpec(memory_space=pltpu.SMEM)]
        + [pl.BlockSpec(memory_space=pltpu.VMEM)] * blocks,
        out_specs=pl.BlockSpec(memory_space=pltpu.HBM),
        out_shape=jax.ShapeDtypeStruct((members, blocks, entries), parts[0].dtype),
        scratch_shapes=[
            pltpu.VMEM((blocks, MEMBER_TILE, width), parts[0].dtype),
            pltpu.VMEM((members, blocks, width), parts[0].dtype),
            pltpu.SemaphoreType.DMA((members // MEMBER_TILE,)),
        ],
        compiler_params=pltpu.CompilerParams(vmem_limit_bytes=16 * MIB),
        cost_estimate=pl.CostEstimate(
            flops=0, bytes_accessed=4 * members * blocks * width, transcendentals=0
        ),
        name=name,
    )(place, *parts)


def transform_kernel(place_ref, tally_ref, weight_ref, innov_ref, *refs):
    *part_refs, out_ref, obs_ref = refs[:-8]
    weighted, precision, root, step, root_next, step_next, inverse, arrived = refs[-8:]
    count_k, slots = obs_ref.shape
    members = count_k // len(part_refs)
    copies = []
    for number, ref in enumerate(part_refs):
        at = pl.multiple_of((place_ref[0] ^ number) * members, members)
        copies.append(
            pltpu.make_async_copy(ref, obs_ref.at[pl.ds(at, members)], arrived.at[number])
        )
    for copy in copies:
        copy.start()
    for copy in copies:
        copy.wait()
    spare = count_k - 1.0
    chunks = count_k // TRANSFORM_CHUNK
    live = lax.broadcasted_iota(jnp.int32, (1, slots), 1) < tally_ref[0, 0]
    obs_weight = jnp.where(live, weight_ref[...], 0.0)

    def span(chunk):
        return pl.ds(pl.multiple_of(chunk * TRANSFORM_CHUNK, TRANSFORM_CHUNK), TRANSFORM_CHUNK)

    def on_diagonal(chunk, value):
        rows = lax.broadcasted_iota(jnp.int32, (count_k, TRANSFORM_CHUNK), 0)
        columns = lax.broadcasted_iota(jnp.int32, (count_k, TRANSFORM_CHUNK), 1)
        return jnp.where(rows == columns + chunk * TRANSFORM_CHUNK, value, 0.0)

    def matmul(left, right):
        return jnp.dot(left, right, preferred_element_type=jnp.float32)

    def by_rows(left, right):
        return lax.dot_general(
            left, right, (((1,), (1,)), ((), ())), preferred_element_type=jnp.float32
        )

    def precise(row, matrix):
        high = row.astype(jnp.bfloat16)
        rest = row - high.astype(jnp.float32)
        middle = rest.astype(jnp.bfloat16)
        low = (rest - middle.astype(jnp.float32)).astype(jnp.bfloat16)
        return (matmul(low, matrix) + matmul(middle, matrix)) + matmul(high, matrix)

    def weigh(chunk, trace):
        at = span(chunk)
        scaled = (obs_ref[at, :].astype(jnp.float32) * obs_weight).astype(jnp.bfloat16)
        weighted[at, :] = scaled
        product = by_rows(obs_ref[...], scaled)
        precision[:, at] = product
        return trace + jnp.sum(on_diagonal(chunk, product))

    trace = lax.fori_loop(0, chunks, weigh, jnp.float32(0.0))
    trace_mean = trace / count_k + spare
    scale = 1.0 / trace_mean
    gain = by_rows(innov_ref[...], weighted[...])

    @pl.loop(0, chunks)
    def _(chunk):
        at = span(chunk)
        first = ((precision[:, at] + on_diagonal(chunk, spare)) * scale).astype(jnp.bfloat16)
        root[:, at] = first
        step[:, at] = (on_diagonal(chunk, 1.5) - 0.5 * first.astype(jnp.float32)).astype(jnp.bfloat16)

    @pl.loop(0, chunks)
    def _(chunk):
        at = span(chunk)
        root_next[:, at] = matmul(step[...], root[:, at]).astype(jnp.bfloat16)

    @pl.loop(0, chunks)
    def _(chunk):
        at = span(chunk)
        product = matmul(root_next[...], step[:, at])
        step_next[:, at] = (on_diagonal(chunk, 1.5) - 0.5 * product).astype(jnp.bfloat16)

    @pl.loop(0, chunks)
    def _(chunk):
        at = span(chunk)
        inverse[:, at] = matmul(step[...], step_next[:, at]).astype(jnp.bfloat16)

    inner = precise(gain, inverse[...])
    mean_weight = precise(inner, inverse[...])[:1] * scale
    spread_factor = jnp.sqrt(jnp.full((1, slots), spare * scale, jnp.float32))
    out_ref[...] = (
        spread_factor[:, :count_k] * inverse[...].astype(jnp.float32) + mean_weight
    ).astype(jnp.bfloat16)


def ensemble_transform(place, tally, weight, innov, parts):
    members, slots = parts[0].shape
    count_k = members * len(parts)
    vmem = pl.BlockSpec(memory_space=pltpu.VMEM)
    square = pltpu.VMEM((count_k, count_k), jnp.bfloat16)
    return pl.pallas_call(
        transform_kernel,
        in_specs=[pl.BlockSpec(memory_space=pltpu.SMEM)] * 2
        + [vmem] * 2
        + [pl.BlockSpec(memory_space=pl.ANY)] * len(parts),
        out_specs=vmem,
        out_shape=jax.ShapeDtypeStruct((count_k, count_k), jnp.bfloat16),
        scratch_shapes=[
            pltpu.VMEM((count_k, slots), jnp.bfloat16),
            pltpu.VMEM((count_k, slots), jnp.bfloat16),
            pltpu.VMEM((count_k, count_k), jnp.float32),
            square, square, square, square, square,
            pltpu.SemaphoreType.DMA((len(parts),)),
        ],
        compiler_params=pltpu.CompilerParams(vmem_limit_bytes=40 * MIB),
        cost_estimate=pl.CostEstimate(
            flops=0,
            bytes_accessed=count_k * slots,
            transcendentals=0,
        ),
        name="transform",
    )(place, tally, weight, innov, *parts)


def analysis_kernel(in_pairs, place_ref, transform_ref, state_ref, out_ref, stage):
    blocks, members, width = out_ref.shape
    state = state_ref[...].astype(jnp.float32)
    state_mean = jnp.sum(state, axis=0, keepdims=True) * (1.0 / state.shape[0])
    perturb = (state - state_mean).astype(jnp.bfloat16)
    increment = jnp.dot(transform_ref[...], perturb, preferred_element_type=jnp.float32)
    result = (state_mean + increment).astype(jnp.bfloat16).reshape(out_ref.shape)
    if in_pairs:
        stage[...] = result
        for number in range(blocks):
            out_ref[number] = stage[place_ref[0] ^ number]
    else:
        out_ref[...] = result


def analysed(place, transform, part, in_pairs, name):
    blocks, members, width = part.shape
    count_k = blocks * members
    return pl.pallas_call(
        functools.partial(analysis_kernel, in_pairs),
        grid=(width // ANALYSIS_TILE,),
        in_specs=[
            pl.BlockSpec(memory_space=pltpu.SMEM),
            pl.BlockSpec(memory_space=pltpu.VMEM),
            pl.BlockSpec((count_k, ANALYSIS_TILE), lambda i: (0, i)),
        ],
        out_specs=pl.BlockSpec((blocks, members, ANALYSIS_TILE), lambda i: (0, 0, i)),
        out_shape=jax.ShapeDtypeStruct(part.shape, jnp.bfloat16),
        scratch_shapes=[pltpu.VMEM((blocks, members, ANALYSIS_TILE), jnp.bfloat16)],
        compiler_params=pltpu.CompilerParams(vmem_limit_bytes=32 * MIB),
        cost_estimate=pl.CostEstimate(
            flops=0,
            bytes_accessed=count_k * width,
            transcendentals=0,
        ),
        name=name,
    )(place, transform, part.reshape(count_k, width))


def body(
    prior_members_field,
    measure_space_deviations,
    measured_minus_predicted,
    measure_pool_indices,
    active_measure_tally,
    tapered_error_weight,
):
    place = lax.axis_index("mem").astype(jnp.int32).reshape(1)
    strips = lax.axis_size("reg")
    devices = lax.axis_size("mem")
    entries = prior_members_field.shape[3]
    to_next = [(i, i + 1) for i in range(strips - 1)]
    to_last = [(i + 1, i) for i in range(strips - 1)]

    def exchange(x):
        return lax.all_to_all(x, "mem", split_axis=0, concat_axis=0, tiled=True)

    def swap(x, number):
        return lax.ppermute(x, "mem", [(i, i ^ number) for i in range(devices)])

    half = devices // 2
    width = entries // 2
    state = prior_members_field[:, 0]
    state_a = to_blocks(state, 0, width, "state_a")
    devs, state_a = lax.optimization_barrier((measure_space_deviations[:, 0], state_a))
    state_a = exchange(state_a)
    pool = pool_rows(devs, measured_minus_predicted[0])
    up = lax.ppermute(pool, "reg", to_next)
    down = lax.ppermute(pool, "reg", to_last)
    picks = measure_pool_indices[0]
    far = gather_chosen(place, pool, up, down, picks, half, half, "gather_far")[0]
    pool, far = lax.optimization_barrier((pool, far))
    far = [swap(far[k], k + half) for k in range(half)]
    near, innov = gather_chosen(place, pool, up, down, picks, 0, half, "gather_near")
    near = [near[0]] + [swap(near[k], k) for k in range(1, half)]
    state_b = to_blocks(state, width, entries - width, "state_b")
    near, far, state_a, state_b = lax.optimization_barrier((near, far, state_a, state_b))
    state_b = exchange(state_b)
    transform = ensemble_transform(
        place, active_measure_tally, tapered_error_weight[0], innov, near + far
    )
    done_a = analysed(place, transform, state_a, True, "analysed_a")
    transform, done_a = lax.optimization_barrier((transform, done_a))
    done_a = [done_a[0]] + [swap(done_a[k], k) for k in range(1, devices)]
    done_b = analysed(place, transform, state_b, False, "analysed_b")
    done_b, *done_a[half : half + 2] = lax.optimization_barrier(
        (done_b, *done_a[half : half + 2])
    )
    done_b = exchange(done_b)
    whole = pairs_to_members(place, done_a, 0, entries, "analysis_a")
    whole = to_members(done_b, width, whole, "analysis_b")
    return whole[:, None]


def solution(mesh):
    in_specs = (
        P("mem", "reg", None, None),
        P("mem", "reg", None, None),
        P("reg", None, None),
        P("reg", None, None),
        P("reg", "mem"),
        P("reg", "mem", None),
    )
    out_specs = P("mem", "reg", None, None)
    return jax.shard_map(body, mesh=mesh, in_specs=in_specs, out_specs=out_specs, check_vma=False)
```

```python
import functools

import jax
import jax.numpy as jnp
from jax import lax
from jax.experimental import pallas as pl
from jax.experimental.pallas import tpu as pltpu
from jax.sharding import PartitionSpec as P

INNOV_ROWS = 16
SLOT_CHUNK = 256
MEMBER_TILE = 32
TRANSFORM_CHUNK = 256
ANALYSIS_TILE = 128
MIB = 1024 * 1024


def fetch_tiles(source_ref, start, stage, arrived, use):
    width = stage.shape[2]
    tiles = []
    for number in range(stage.shape[0] // MEMBER_TILE):
        rows = pl.ds(number * MEMBER_TILE, MEMBER_TILE)
        copy = pltpu.make_async_copy(
            source_ref.at[rows, :, pl.ds(start, width)], stage.at[rows], arrived.at[number]
        )
        copy.start()
        tiles.append((copy, rows))
    for copy, rows in tiles:
        copy.wait()
        use(rows)


def to_blocks_kernel(start, state_ref, out_ref, stage, arrived):
    def use(rows):
        out_ref[:, rows, :] = jnp.swapaxes(stage[rows], 0, 1)

    fetch_tiles(state_ref, start, stage, arrived, use)


def to_blocks(state, start, width, name):
    members, blocks, _ = state.shape
    return pl.pallas_call(
        functools.partial(to_blocks_kernel, start),
        in_specs=[pl.BlockSpec(memory_space=pltpu.HBM)],
        out_specs=pl.BlockSpec(memory_space=pltpu.VMEM),
        out_shape=jax.ShapeDtypeStruct((blocks, members, width), state.dtype),
        scratch_shapes=[
            pltpu.VMEM((members, blocks, width), state.dtype),
            pltpu.SemaphoreType.DMA((members // MEMBER_TILE,)),
        ],
        compiler_params=pltpu.CompilerParams(vmem_limit_bytes=60 * MIB),
        cost_estimate=pl.CostEstimate(
            flops=0, bytes_accessed=4 * members * blocks * width, transcendentals=0
        ),
        name=name,
    )(state)


def pool_kernel(obs_ref, innov_ref, out_ref, stage, arrived):
    members = obs_ref.shape[0]

    def use(rows):
        out_ref[:, rows, :] = jnp.swapaxes(stage[rows], 0, 1)

    shape = (out_ref.shape[0], INNOV_ROWS, out_ref.shape[2])
    out_ref[:, members:, :] = jnp.broadcast_to(innov_ref[...][:, None, :], shape)
    fetch_tiles(obs_ref, 0, stage, arrived, use)


def pool_rows(obs, innov):
    members, blocks, depth = obs.shape
    rows = members + INNOV_ROWS
    vmem = pl.BlockSpec(memory_space=pltpu.VMEM)
    return pl.pallas_call(
        pool_kernel,
        in_specs=[pl.BlockSpec(memory_space=pltpu.HBM), vmem],
        out_specs=vmem,
        out_shape=jax.ShapeDtypeStruct((blocks, rows, depth), obs.dtype),
        scratch_shapes=[
            pltpu.VMEM((members, blocks, depth), obs.dtype),
            pltpu.SemaphoreType.DMA((members // MEMBER_TILE,)),
        ],
        compiler_params=pltpu.CompilerParams(vmem_limit_bytes=60 * MIB),
        cost_estimate=pl.CostEstimate(
            flops=0, bytes_accessed=4 * rows * blocks * depth, transcendentals=0
        ),
        name="pool_rows",
    )(obs, innov)


def gather_kernel(place_ref, own_ref, up_ref, down_ref, idx_ref, out_ref, inn_ref, stacked):
    block = pl.program_id(0) ^ place_ref[0]
    blocks, rows, depth = own_ref.shape
    members = out_ref.shape[1]
    slots = out_ref.shape[2]
    west = jnp.maximum(block - 1, 0)
    east = jnp.minimum(block + 1, blocks - 1)
    sources = (
        own_ref[block, :rows],
        up_ref[block, :rows],
        down_ref[block, :rows],
        jnp.where(block > 0, own_ref[west, :rows], 0.0),
        jnp.where(block < blocks - 1, own_ref[east, :rows], 0.0),
    )
    for number, source in enumerate(sources):
        stacked[number * rows : (number + 1) * rows] = source.astype(jnp.bfloat16)
    columns = lax.broadcasted_iota(jnp.int32, (depth, SLOT_CHUNK), 0)

    @pl.loop(0, slots // SLOT_CHUNK)
    def _(chunk):
        where = pl.ds(pl.multiple_of(chunk * SLOT_CHUNK, SLOT_CHUNK), SLOT_CHUNK)
        picks = idx_ref[pl.ds(block, 1), where]
        source = sum((picks >= number * depth).astype(jnp.int32) for number in range(1, 5))
        one_hot = jnp.where(columns == picks - source * depth, 1.0, 0.0).astype(jnp.bfloat16)
        products = jnp.dot(stacked[...], one_hot, preferred_element_type=jnp.float32)
        chosen = products[:rows]
        for number in range(1, 5):
            part = products[number * rows : (number + 1) * rows]
            chosen = jnp.where(source == number, part, chosen)
        out_ref[0, :, where] = chosen[:members].astype(jnp.bfloat16)

        @pl.when(pl.program_id(0) == 0)
        def _():
            inn_ref[:, where] = chosen[members:].astype(jnp.bfloat16)


def gather_chosen(place, own, up, down, picks):
    blocks, rows, depth = own.shape
    members = rows - INNOV_ROWS
    slots = picks.shape[1]
    vmem = pl.BlockSpec(memory_space=pltpu.VMEM)
    return pl.pallas_call(
        gather_kernel,
        grid=(blocks,),
        in_specs=[pl.BlockSpec(memory_space=pltpu.SMEM)] + [vmem] * 4,
        out_specs=[
            pl.BlockSpec((1, members, slots), lambda k: (k, 0, 0)),
            pl.BlockSpec((INNOV_ROWS, slots), lambda k: (0, 0)),
        ],
        out_shape=[
            jax.ShapeDtypeStruct((blocks, members, slots), jnp.bfloat16),
            jax.ShapeDtypeStruct((INNOV_ROWS, slots), jnp.bfloat16),
        ],
        scratch_shapes=[pltpu.VMEM((5 * rows, depth), jnp.bfloat16)],
        compiler_params=pltpu.CompilerParams(vmem_limit_bytes=40 * MIB),
        cost_estimate=pl.CostEstimate(flops=0, bytes_accessed=rows * slots, transcendentals=0),
        name="gather_chosen",
    )(place, own, up, down, picks)


def store_tiles(out_ref, start, stage, sent, make):
    width = stage.shape[2]
    copies = []
    for number in range(stage.shape[0] // MEMBER_TILE):
        rows = pl.ds(number * MEMBER_TILE, MEMBER_TILE)
        stage[rows] = make(rows)
        copy = pltpu.make_async_copy(
            stage.at[rows], out_ref.at[rows, :, pl.ds(start, width)], sent.at[number]
        )
        copy.start()
        copies.append(copy)
    for copy in copies:
        copy.wait()


def to_members_kernel(start, part_ref, out_ref, stage, sent):
    store_tiles(out_ref, start, stage, sent, lambda rows: jnp.swapaxes(part_ref[:, rows, :], 0, 1))


def pairs_to_members_kernel(start, place_ref, whole_ref, *refs):
    *part_refs, out_ref, turned, stage, sent = refs
    del whole_ref

    def make(rows):
        for number, ref in enumerate(part_refs):
            turned[place_ref[0] ^ number] = ref[rows]
        return jnp.swapaxes(turned[...], 0, 1)

    store_tiles(out_ref, start, stage, sent, make)


def to_members(part, start, entries, name):
    blocks, members, width = part.shape
    return pl.pallas_call(
        functools.partial(to_members_kernel, start),
        in_specs=[pl.BlockSpec(memory_space=pltpu.VMEM)],
        out_specs=pl.BlockSpec(memory_space=pltpu.HBM),
        out_shape=jax.ShapeDtypeStruct((members, blocks, entries), part.dtype),
        scratch_shapes=[
            pltpu.VMEM((members, blocks, width), part.dtype),
            pltpu.SemaphoreType.DMA((members // MEMBER_TILE,)),
        ],
        compiler_params=pltpu.CompilerParams(vmem_limit_bytes=16 * MIB),
        cost_estimate=pl.CostEstimate(
            flops=0, bytes_accessed=4 * members * blocks * width, transcendentals=0
        ),
        name=name,
    )(part)


def pairs_to_members(place, parts, start, whole, name):
    blocks = len(parts)
    members, width = parts[0].shape
    hbm = pl.BlockSpec(memory_space=pltpu.HBM)
    return pl.pallas_call(
        functools.partial(pairs_to_members_kernel, start),
        in_specs=[pl.BlockSpec(memory_space=pltpu.SMEM), hbm]
        + [pl.BlockSpec(memory_space=pltpu.VMEM)] * blocks,
        out_specs=hbm,
        out_shape=jax.ShapeDtypeStruct(whole.shape, whole.dtype),
        scratch_shapes=[
            pltpu.VMEM((blocks, MEMBER_TILE, width), whole.dtype),
            pltpu.VMEM((members, blocks, width), whole.dtype),
            pltpu.SemaphoreType.DMA((members // MEMBER_TILE,)),
        ],
        input_output_aliases={1: 0},
        compiler_params=pltpu.CompilerParams(vmem_limit_bytes=16 * MIB),
        cost_estimate=pl.CostEstimate(
            flops=0, bytes_accessed=4 * members * blocks * width, transcendentals=0
        ),
        name=name,
    )(place, whole, *parts)


def transform_kernel(place_ref, tally_ref, weight_ref, innov_ref, *refs):
    *part_refs, out_ref, obs_ref = refs[:-8]
    weighted, precision, root, step, root_next, step_next, inverse, arrived = refs[-8:]
    count_k, slots = obs_ref.shape
    members = count_k // len(part_refs)
    copies = []
    for number, ref in enumerate(part_refs):
        at = pl.multiple_of((place_ref[0] ^ number) * members, members)
        copies.append(
            pltpu.make_async_copy(ref, obs_ref.at[pl.ds(at, members)], arrived.at[number])
        )
    for copy in copies:
        copy.start()
    for copy in copies:
        copy.wait()
    spare = count_k - 1.0
    chunks = count_k // TRANSFORM_CHUNK
    live = lax.broadcasted_iota(jnp.int32, (1, slots), 1) < tally_ref[0, 0]
    obs_weight = jnp.where(live, weight_ref[...], 0.0)

    def span(chunk):
        return pl.ds(pl.multiple_of(chunk * TRANSFORM_CHUNK, TRANSFORM_CHUNK), TRANSFORM_CHUNK)

    def on_diagonal(chunk, value):
        rows = lax.broadcasted_iota(jnp.int32, (count_k, TRANSFORM_CHUNK), 0)
        columns = lax.broadcasted_iota(jnp.int32, (count_k, TRANSFORM_CHUNK), 1)
        return jnp.where(rows == columns + chunk * TRANSFORM_CHUNK, value, 0.0)

    def matmul(left, right):
        return jnp.dot(left, right, preferred_element_type=jnp.float32)

    def by_rows(left, right):
        return lax.dot_general(
            left, right, (((1,), (1,)), ((), ())), preferred_element_type=jnp.float32
        )

    def precise(row, matrix):
        high = row.astype(jnp.bfloat16)
        rest = row - high.astype(jnp.float32)
        middle = rest.astype(jnp.bfloat16)
        low = (rest - middle.astype(jnp.float32)).astype(jnp.bfloat16)
        return (matmul(low, matrix) + matmul(middle, matrix)) + matmul(high, matrix)

    def weigh(chunk, trace):
        at = span(chunk)
        scaled = (obs_ref[at, :].astype(jnp.float32) * obs_weight).astype(jnp.bfloat16)
        weighted[at, :] = scaled
        product = by_rows(obs_ref[...], scaled)
        precision[:, at] = product
        return trace + jnp.sum(on_diagonal(chunk, product))

    trace = lax.fori_loop(0, chunks, weigh, jnp.float32(0.0))
    trace_mean = trace / count_k + spare
    scale = 1.0 / trace_mean
    gain = by_rows(innov_ref[...], weighted[...])

    @pl.loop(0, chunks)
    def _(chunk):
        at = span(chunk)
        first = ((precision[:, at] + on_diagonal(chunk, spare)) * scale).astype(jnp.bfloat16)
        root[:, at] = first
        step[:, at] = (on_diagonal(chunk, 1.5) - 0.5 * first.astype(jnp.float32)).astype(jnp.bfloat16)

    @pl.loop(0, chunks)
    def _(chunk):
        at = span(chunk)
        root_next[:, at] = matmul(step[...], root[:, at]).astype(jnp.bfloat16)

    @pl.loop(0, chunks)
    def _(chunk):
        at = span(chunk)
        product = matmul(root_next[...], step[:, at])
        step_next[:, at] = (on_diagonal(chunk, 1.5) - 0.5 * product).astype(jnp.bfloat16)

    @pl.loop(0, chunks)
    def _(chunk):
        at = span(chunk)
        inverse[:, at] = matmul(step[...], step_next[:, at]).astype(jnp.bfloat16)

    inner = precise(gain, inverse[...])
    mean_weight = precise(inner, inverse[...])[:1] * scale
    spread_factor = jnp.sqrt(jnp.full((1, slots), spare * scale, jnp.float32))
    out_ref[...] = (
        spread_factor[:, :count_k] * inverse[...].astype(jnp.float32) + mean_weight
    ).astype(jnp.bfloat16)


def ensemble_transform(place, tally, weight, innov, parts):
    members, slots = parts[0].shape
    count_k = members * len(parts)
    vmem = pl.BlockSpec(memory_space=pltpu.VMEM)
    square = pltpu.VMEM((count_k, count_k), jnp.bfloat16)
    return pl.pallas_call(
        transform_kernel,
        in_specs=[pl.BlockSpec(memory_space=pltpu.SMEM)] * 2
        + [vmem] * 2
        + [pl.BlockSpec(memory_space=pl.ANY)] * len(parts),
        out_specs=vmem,
        out_shape=jax.ShapeDtypeStruct((count_k, count_k), jnp.bfloat16),
        scratch_shapes=[
            pltpu.VMEM((count_k, slots), jnp.bfloat16),
            pltpu.VMEM((count_k, slots), jnp.bfloat16),
            pltpu.VMEM((count_k, count_k), jnp.float32),
            square, square, square, square, square,
            pltpu.SemaphoreType.DMA((len(parts),)),
        ],
        compiler_params=pltpu.CompilerParams(vmem_limit_bytes=40 * MIB),
        cost_estimate=pl.CostEstimate(
            flops=0,
            bytes_accessed=count_k * slots,
            transcendentals=0,
        ),
        name="transform",
    )(place, tally, weight, innov, *parts)


def analysis_kernel(in_pairs, place_ref, transform_ref, state_ref, out_ref, stage):
    blocks, members, width = out_ref.shape
    state = state_ref[...].astype(jnp.float32)
    state_mean = jnp.sum(state, axis=0, keepdims=True) * (1.0 / state.shape[0])
    perturb = (state - state_mean).astype(jnp.bfloat16)
    increment = jnp.dot(transform_ref[...], perturb, preferred_element_type=jnp.float32)
    result = (state_mean + increment).astype(jnp.bfloat16).reshape(out_ref.shape)
    if in_pairs:
        stage[...] = result
        for number in range(blocks):
            out_ref[number] = stage[place_ref[0] ^ number]
    else:
        out_ref[...] = result


def analysed(place, transform, part, in_pairs, name):
    blocks, members, width = part.shape
    count_k = blocks * members
    return pl.pallas_call(
        functools.partial(analysis_kernel, in_pairs),
        grid=(width // ANALYSIS_TILE,),
        in_specs=[
            pl.BlockSpec(memory_space=pltpu.SMEM),
            pl.BlockSpec(memory_space=pltpu.VMEM),
            pl.BlockSpec((count_k, ANALYSIS_TILE), lambda i: (0, i)),
        ],
        out_specs=pl.BlockSpec((blocks, members, ANALYSIS_TILE), lambda i: (0, 0, i)),
        out_shape=jax.ShapeDtypeStruct(part.shape, jnp.bfloat16),
        scratch_shapes=[pltpu.VMEM((blocks, members, ANALYSIS_TILE), jnp.bfloat16)],
        compiler_params=pltpu.CompilerParams(vmem_limit_bytes=32 * MIB),
        cost_estimate=pl.CostEstimate(
            flops=0,
            bytes_accessed=count_k * width,
            transcendentals=0,
        ),
        name=name,
    )(place, transform, part.reshape(count_k, width))


def body(
    prior_members_field,
    measure_space_deviations,
    measured_minus_predicted,
    measure_pool_indices,
    active_measure_tally,
    tapered_error_weight,
):
    place = lax.axis_index("mem").astype(jnp.int32).reshape(1)
    strips = lax.axis_size("reg")
    devices = lax.axis_size("mem")
    entries = prior_members_field.shape[3]
    to_next = [(i, i + 1) for i in range(strips - 1)]
    to_last = [(i + 1, i) for i in range(strips - 1)]

    def exchange(x):
        return lax.all_to_all(x, "mem", split_axis=0, concat_axis=0, tiled=True)

    def swap(x, number):
        return lax.ppermute(x, "mem", [(i, i ^ number) for i in range(devices)])

    half = devices // 2
    width = entries // 2
    state = prior_members_field[:, 0]
    state_a = to_blocks(state, 0, width, "state_a")
    devs, state_a = lax.optimization_barrier((measure_space_deviations[:, 0], state_a))
    state_a = exchange(state_a)
    pool = pool_rows(devs, measured_minus_predicted[0])
    up = lax.ppermute(pool, "reg", to_next)
    down = lax.ppermute(pool, "reg", to_last)
    chosen, innov = gather_chosen(place, pool, up, down, measure_pool_indices[0])
    far = [swap(chosen[k], k) for k in range(half, devices)]
    near = [chosen[0]] + [swap(chosen[k], k) for k in range(1, half)]
    state_b = to_blocks(state, width, entries - width, "state_b")
    near, far, state_a, state_b = lax.optimization_barrier((near, far, state_a, state_b))
    state_b = exchange(state_b)
    transform = ensemble_transform(
        place, active_measure_tally, tapered_error_weight[0], innov, near + far
    )
    done_a = analysed(place, transform, state_a, True, "analysed_a")
    transform, done_a = lax.optimization_barrier((transform, done_a))
    done_a = [done_a[0]] + [swap(done_a[k], k) for k in range(1, devices)]
    done_b = analysed(place, transform, state_b, False, "analysed_b")
    done_b, *done_a[half : half + 2] = lax.optimization_barrier(
        (done_b, *done_a[half : half + 2])
    )
    done_b = exchange(done_b)
    whole = to_members(done_b, width, entries, "analysis_b")
    whole = pairs_to_members(place, done_a, 0, whole, "analysis_a")
    return whole[:, None]


def solution(mesh):
    in_specs = (
        P("mem", "reg", None, None),
        P("mem", "reg", None, None),
        P("reg", None, None),
        P("reg", None, None),
        P("reg", "mem"),
        P("reg", "mem", None),
    )
    out_specs = P("mem", "reg", None, None)
    return jax.shard_map(body, mesh=mesh, in_specs=in_specs, out_specs=out_specs, check_vma=False)
```

```python
import functools

import jax
import jax.numpy as jnp
from jax import lax
from jax.experimental import pallas as pl
from jax.experimental.pallas import tpu as pltpu
from jax.sharding import PartitionSpec as P

INNOV_ROWS = 16
SLOT_CHUNK = 256
MEMBER_TILE = 32
TRANSFORM_CHUNK = 256
ANALYSIS_TILE = 128
MIB = 1024 * 1024


def fetch_tiles(source_ref, start, stage, arrived, use):
    width = stage.shape[2]
    tiles = []
    for number in range(stage.shape[0] // MEMBER_TILE):
        rows = pl.ds(number * MEMBER_TILE, MEMBER_TILE)
        copy = pltpu.make_async_copy(
            source_ref.at[rows, :, pl.ds(start, width)], stage.at[rows], arrived.at[number]
        )
        copy.start()
        tiles.append((copy, rows))
    for copy, rows in tiles:
        copy.wait()
        use(rows)


def to_blocks_kernel(start, state_ref, out_ref, stage, turned, arrived, sent):
    stores = []

    def use(rows):
        turned[:, rows, :] = jnp.swapaxes(stage[rows], 0, 1)
        store = pltpu.make_async_copy(
            turned.at[:, rows, :], out_ref.at[:, rows, :], sent.at[len(stores)]
        )
        store.start()
        stores.append(store)

    fetch_tiles(state_ref, start, stage, arrived, use)
    for store in stores:
        store.wait()


def to_blocks(state, start, width, name):
    members, blocks, _ = state.shape
    hbm = pl.BlockSpec(memory_space=pltpu.HBM)
    return pl.pallas_call(
        functools.partial(to_blocks_kernel, start),
        in_specs=[hbm],
        out_specs=hbm,
        out_shape=jax.ShapeDtypeStruct((blocks, members, width), state.dtype),
        scratch_shapes=[
            pltpu.VMEM((members, blocks, width), state.dtype),
            pltpu.VMEM((blocks, members, width), state.dtype),
            pltpu.SemaphoreType.DMA((members // MEMBER_TILE,)),
            pltpu.SemaphoreType.DMA((members // MEMBER_TILE,)),
        ],
        compiler_params=pltpu.CompilerParams(vmem_limit_bytes=60 * MIB),
        cost_estimate=pl.CostEstimate(
            flops=0, bytes_accessed=4 * members * blocks * width, transcendentals=0
        ),
        name=name,
    )(state)


def pool_kernel(obs_ref, innov_ref, out_ref, stage, arrived):
    members = obs_ref.shape[0]

    def use(rows):
        out_ref[:, rows, :] = jnp.swapaxes(stage[rows], 0, 1)

    shape = (out_ref.shape[0], INNOV_ROWS, out_ref.shape[2])
    out_ref[:, members:, :] = jnp.broadcast_to(innov_ref[...][:, None, :], shape)
    fetch_tiles(obs_ref, 0, stage, arrived, use)


def pool_rows(obs, innov):
    members, blocks, depth = obs.shape
    rows = members + INNOV_ROWS
    vmem = pl.BlockSpec(memory_space=pltpu.VMEM)
    return pl.pallas_call(
        pool_kernel,
        in_specs=[pl.BlockSpec(memory_space=pltpu.HBM), vmem],
        out_specs=vmem,
        out_shape=jax.ShapeDtypeStruct((blocks, rows, depth), obs.dtype),
        scratch_shapes=[
            pltpu.VMEM((members, blocks, depth), obs.dtype),
            pltpu.SemaphoreType.DMA((members // MEMBER_TILE,)),
        ],
        compiler_params=pltpu.CompilerParams(vmem_limit_bytes=60 * MIB),
        cost_estimate=pl.CostEstimate(
            flops=0, bytes_accessed=4 * rows * blocks * depth, transcendentals=0
        ),
        name="pool_rows",
    )(obs, innov)


def gather_kernel(place_ref, own_ref, up_ref, down_ref, idx_ref, out_ref, inn_ref, stacked):
    block = pl.program_id(0) ^ place_ref[0]
    blocks, rows, depth = own_ref.shape
    members = out_ref.shape[1]
    slots = out_ref.shape[2]
    west = jnp.maximum(block - 1, 0)
    east = jnp.minimum(block + 1, blocks - 1)
    sources = (
        own_ref[block, :rows],
        up_ref[block, :rows],
        down_ref[block, :rows],
        jnp.where(block > 0, own_ref[west, :rows], 0.0),
        jnp.where(block < blocks - 1, own_ref[east, :rows], 0.0),
    )
    for number, source in enumerate(sources):
        stacked[number * rows : (number + 1) * rows] = source.astype(jnp.bfloat16)
    columns = lax.broadcasted_iota(jnp.int32, (depth, SLOT_CHUNK), 0)

    @pl.loop(0, slots // SLOT_CHUNK)
    def _(chunk):
        where = pl.ds(pl.multiple_of(chunk * SLOT_CHUNK, SLOT_CHUNK), SLOT_CHUNK)
        picks = idx_ref[pl.ds(block, 1), where]
        source = sum((picks >= number * depth).astype(jnp.int32) for number in range(1, 5))
        one_hot = jnp.where(columns == picks - source * depth, 1.0, 0.0).astype(jnp.bfloat16)
        products = jnp.dot(stacked[...], one_hot, preferred_element_type=jnp.float32)
        chosen = products[:rows]
        for number in range(1, 5):
            part = products[number * rows : (number + 1) * rows]
            chosen = jnp.where(source == number, part, chosen)
        out_ref[0, :, where] = chosen[:members].astype(jnp.bfloat16)

        @pl.when(pl.program_id(0) == 0)
        def _():
            inn_ref[:, where] = chosen[members:].astype(jnp.bfloat16)


def gather_chosen(place, own, up, down, picks):
    blocks, rows, depth = own.shape
    members = rows - INNOV_ROWS
    slots = picks.shape[1]
    vmem = pl.BlockSpec(memory_space=pltpu.VMEM)
    return pl.pallas_call(
        gather_kernel,
        grid=(blocks,),
        in_specs=[pl.BlockSpec(memory_space=pltpu.SMEM)] + [vmem] * 4,
        out_specs=[
            pl.BlockSpec((1, members, slots), lambda k: (k, 0, 0)),
            pl.BlockSpec((INNOV_ROWS, slots), lambda k: (0, 0)),
        ],
        out_shape=[
            jax.ShapeDtypeStruct((blocks, members, slots), jnp.bfloat16),
            jax.ShapeDtypeStruct((INNOV_ROWS, slots), jnp.bfloat16),
        ],
        scratch_shapes=[pltpu.VMEM((5 * rows, depth), jnp.bfloat16)],
        compiler_params=pltpu.CompilerParams(vmem_limit_bytes=40 * MIB),
        cost_estimate=pl.CostEstimate(flops=0, bytes_accessed=rows * slots, transcendentals=0),
        name="gather_chosen",
    )(place, own, up, down, picks)


def store_tiles(out_ref, start, stage, sent, make):
    width = stage.shape[2]
    copies = []
    for number in range(stage.shape[0] // MEMBER_TILE):
        rows = pl.ds(number * MEMBER_TILE, MEMBER_TILE)
        stage[rows] = make(rows)
        copy = pltpu.make_async_copy(
            stage.at[rows], out_ref.at[rows, :, pl.ds(start, width)], sent.at[number]
        )
        copy.start()
        copies.append(copy)
    for copy in copies:
        copy.wait()


def to_members_kernel(start, part_ref, out_ref, stage, sent):
    store_tiles(out_ref, start, stage, sent, lambda rows: jnp.swapaxes(part_ref[:, rows, :], 0, 1))


def pairs_to_members_kernel(start, place_ref, whole_ref, *refs):
    *part_refs, out_ref, turned, stage, sent = refs
    del whole_ref

    def make(rows):
        for number, ref in enumerate(part_refs):
            turned[place_ref[0] ^ number] = ref[rows]
        return jnp.swapaxes(turned[...], 0, 1)

    store_tiles(out_ref, start, stage, sent, make)


def to_members(part, start, entries, name):
    blocks, members, width = part.shape
    return pl.pallas_call(
        functools.partial(to_members_kernel, start),
        in_specs=[pl.BlockSpec(memory_space=pltpu.VMEM)],
        out_specs=pl.BlockSpec(memory_space=pltpu.HBM),
        out_shape=jax.ShapeDtypeStruct((members, blocks, entries), part.dtype),
        scratch_shapes=[
            pltpu.VMEM((members, blocks, width), part.dtype),
            pltpu.SemaphoreType.DMA((members // MEMBER_TILE,)),
        ],
        compiler_params=pltpu.CompilerParams(vmem_limit_bytes=16 * MIB),
        cost_estimate=pl.CostEstimate(
            flops=0, bytes_accessed=4 * members * blocks * width, transcendentals=0
        ),
        name=name,
    )(part)


def pairs_to_members(place, parts, start, whole, name):
    blocks = len(parts)
    members, width = parts[0].shape
    hbm = pl.BlockSpec(memory_space=pltpu.HBM)
    return pl.pallas_call(
        functools.partial(pairs_to_members_kernel, start),
        in_specs=[pl.BlockSpec(memory_space=pltpu.SMEM), hbm]
        + [pl.BlockSpec(memory_space=pltpu.VMEM)] * blocks,
        out_specs=hbm,
        out_shape=jax.ShapeDtypeStruct(whole.shape, whole.dtype),
        scratch_shapes=[
            pltpu.VMEM((blocks, MEMBER_TILE, width), whole.dtype),
            pltpu.VMEM((members, blocks, width), whole.dtype),
            pltpu.SemaphoreType.DMA((members // MEMBER_TILE,)),
        ],
        input_output_aliases={1: 0},
        compiler_params=pltpu.CompilerParams(vmem_limit_bytes=16 * MIB),
        cost_estimate=pl.CostEstimate(
            flops=0, bytes_accessed=4 * members * blocks * width, transcendentals=0
        ),
        name=name,
    )(place, whole, *parts)


def transform_kernel(place_ref, tally_ref, weight_ref, innov_ref, *refs):
    *part_refs, out_ref, obs_ref = refs[:-8]
    weighted, precision, root, step, root_next, step_next, inverse, arrived = refs[-8:]
    count_k, slots = obs_ref.shape
    members = count_k // len(part_refs)
    copies = []
    for number, ref in enumerate(part_refs):
        at = pl.multiple_of((place_ref[0] ^ number) * members, members)
        copies.append(
            pltpu.make_async_copy(ref, obs_ref.at[pl.ds(at, members)], arrived.at[number])
        )
    for copy in copies:
        copy.start()
    for copy in copies:
        copy.wait()
    spare = count_k - 1.0
    chunks = count_k // TRANSFORM_CHUNK
    live = lax.broadcasted_iota(jnp.int32, (1, slots), 1) < tally_ref[0, 0]
    obs_weight = jnp.where(live, weight_ref[...], 0.0)

    def span(chunk):
        return pl.ds(pl.multiple_of(chunk * TRANSFORM_CHUNK, TRANSFORM_CHUNK), TRANSFORM_CHUNK)

    def on_diagonal(chunk, value):
        rows = lax.broadcasted_iota(jnp.int32, (count_k, TRANSFORM_CHUNK), 0)
        columns = lax.broadcasted_iota(jnp.int32, (count_k, TRANSFORM_CHUNK), 1)
        return jnp.where(rows == columns + chunk * TRANSFORM_CHUNK, value, 0.0)

    def matmul(left, right):
        return jnp.dot(left, right, preferred_element_type=jnp.float32)

    def by_rows(left, right):
        return lax.dot_general(
            left, right, (((1,), (1,)), ((), ())), preferred_element_type=jnp.float32
        )

    def precise(row, matrix):
        high = row.astype(jnp.bfloat16)
        rest = row - high.astype(jnp.float32)
        middle = rest.astype(jnp.bfloat16)
        low = (rest - middle.astype(jnp.float32)).astype(jnp.bfloat16)
        return (matmul(low, matrix) + matmul(middle, matrix)) + matmul(high, matrix)

    def weigh(chunk, trace):
        at = span(chunk)
        scaled = (obs_ref[at, :].astype(jnp.float32) * obs_weight).astype(jnp.bfloat16)
        weighted[at, :] = scaled
        product = by_rows(obs_ref[...], scaled)
        precision[:, at] = product
        return trace + jnp.sum(on_diagonal(chunk, product))

    trace = lax.fori_loop(0, chunks, weigh, jnp.float32(0.0))
    trace_mean = trace / count_k + spare
    scale = 1.0 / trace_mean
    gain = by_rows(innov_ref[...], weighted[...])

    @pl.loop(0, chunks)
    def _(chunk):
        at = span(chunk)
        first = ((precision[:, at] + on_diagonal(chunk, spare)) * scale).astype(jnp.bfloat16)
        root[:, at] = first
        step[:, at] = (on_diagonal(chunk, 1.5) - 0.5 * first.astype(jnp.float32)).astype(jnp.bfloat16)

    @pl.loop(0, chunks)
    def _(chunk):
        at = span(chunk)
        root_next[:, at] = matmul(step[...], root[:, at]).astype(jnp.bfloat16)

    @pl.loop(0, chunks)
    def _(chunk):
        at = span(chunk)
        product = matmul(root_next[...], step[:, at])
        step_next[:, at] = (on_diagonal(chunk, 1.5) - 0.5 * product).astype(jnp.bfloat16)

    @pl.loop(0, chunks)
    def _(chunk):
        at = span(chunk)
        inverse[:, at] = matmul(step[...], step_next[:, at]).astype(jnp.bfloat16)

    inner = precise(gain, inverse[...])
    mean_weight = precise(inner, inverse[...])[:1] * scale
    spread_factor = jnp.sqrt(jnp.full((1, slots), spare * scale, jnp.float32))
    out_ref[...] = (
        spread_factor[:, :count_k] * inverse[...].astype(jnp.float32) + mean_weight
    ).astype(jnp.bfloat16)


def ensemble_transform(place, tally, weight, innov, parts):
    members, slots = parts[0].shape
    count_k = members * len(parts)
    vmem = pl.BlockSpec(memory_space=pltpu.VMEM)
    square = pltpu.VMEM((count_k, count_k), jnp.bfloat16)
    return pl.pallas_call(
        transform_kernel,
        in_specs=[pl.BlockSpec(memory_space=pltpu.SMEM)] * 2
        + [vmem] * 2
        + [pl.BlockSpec(memory_space=pl.ANY)] * len(parts),
        out_specs=vmem,
        out_shape=jax.ShapeDtypeStruct((count_k, count_k), jnp.bfloat16),
        scratch_shapes=[
            pltpu.VMEM((count_k, slots), jnp.bfloat16),
            pltpu.VMEM((count_k, slots), jnp.bfloat16),
            pltpu.VMEM((count_k, count_k), jnp.float32),
            square, square, square, square, square,
            pltpu.SemaphoreType.DMA((len(parts),)),
        ],
        compiler_params=pltpu.CompilerParams(vmem_limit_bytes=40 * MIB),
        cost_estimate=pl.CostEstimate(
            flops=0,
            bytes_accessed=count_k * slots,
            transcendentals=0,
        ),
        name="transform",
    )(place, tally, weight, innov, *parts)


def analysis_kernel(in_pairs, place_ref, transform_ref, state_ref, out_ref, stage):
    blocks, members, width = out_ref.shape
    state = state_ref[...].astype(jnp.float32)
    state_mean = jnp.sum(state, axis=0, keepdims=True) * (1.0 / state.shape[0])
    perturb = (state - state_mean).astype(jnp.bfloat16)
    increment = jnp.dot(transform_ref[...], perturb, preferred_element_type=jnp.float32)
    result = (state_mean + increment).astype(jnp.bfloat16).reshape(out_ref.shape)
    if in_pairs:
        stage[...] = result
        for number in range(blocks):
            out_ref[number] = stage[place_ref[0] ^ number]
    else:
        out_ref[...] = result


def analysed(place, transform, part, in_pairs, name):
    blocks, members, width = part.shape
    count_k = blocks * members
    return pl.pallas_call(
        functools.partial(analysis_kernel, in_pairs),
        grid=(width // ANALYSIS_TILE,),
        in_specs=[
            pl.BlockSpec(memory_space=pltpu.SMEM),
            pl.BlockSpec(memory_space=pltpu.VMEM),
            pl.BlockSpec((count_k, ANALYSIS_TILE), lambda i: (0, i)),
        ],
        out_specs=pl.BlockSpec((blocks, members, ANALYSIS_TILE), lambda i: (0, 0, i)),
        out_shape=jax.ShapeDtypeStruct(part.shape, jnp.bfloat16),
        scratch_shapes=[pltpu.VMEM((blocks, members, ANALYSIS_TILE), jnp.bfloat16)],
        compiler_params=pltpu.CompilerParams(vmem_limit_bytes=32 * MIB),
        cost_estimate=pl.CostEstimate(
            flops=0,
            bytes_accessed=count_k * width,
            transcendentals=0,
        ),
        name=name,
    )(place, transform, part.reshape(count_k, width))


def body(
    prior_members_field,
    measure_space_deviations,
    measured_minus_predicted,
    measure_pool_indices,
    active_measure_tally,
    tapered_error_weight,
):
    place = lax.axis_index("mem").astype(jnp.int32).reshape(1)
    strips = lax.axis_size("reg")
    devices = lax.axis_size("mem")
    entries = prior_members_field.shape[3]
    to_next = [(i, i + 1) for i in range(strips - 1)]
    to_last = [(i + 1, i) for i in range(strips - 1)]

    def exchange(x):
        return lax.all_to_all(x, "mem", split_axis=0, concat_axis=0, tiled=True)

    def swap(x, number):
        return lax.ppermute(x, "mem", [(i, i ^ number) for i in range(devices)])

    half = devices // 2
    width = entries // 2
    state = prior_members_field[:, 0]
    state_a = to_blocks(state, 0, width, "state_a")
    devs, state_a = lax.optimization_barrier((measure_space_deviations[:, 0], state_a))
    state_a = exchange(state_a)
    pool = pool_rows(devs, measured_minus_predicted[0])
    up = lax.ppermute(pool, "reg", to_next)
    down = lax.ppermute(pool, "reg", to_last)
    chosen, innov = gather_chosen(place, pool, up, down, measure_pool_indices[0])
    far = [swap(chosen[k], k) for k in range(half, devices)]
    near = [chosen[0]] + [swap(chosen[k], k) for k in range(1, half)]
    state_b = to_blocks(state, width, entries - width, "state_b")
    near, far, state_a, state_b = lax.optimization_barrier((near, far, state_a, state_b))
    state_b = exchange(state_b)
    transform = ensemble_transform(
        place, active_measure_tally, tapered_error_weight[0], innov, near + far
    )
    done_a = analysed(place, transform, state_a, True, "analysed_a")
    transform, done_a = lax.optimization_barrier((transform, done_a))
    done_a = [done_a[0]] + [swap(done_a[k], k) for k in range(1, devices)]
    done_b = analysed(place, transform, state_b, False, "analysed_b")
    done_b, *done_a[half : half + 2] = lax.optimization_barrier(
        (done_b, *done_a[half : half + 2])
    )
    done_b = exchange(done_b)
    whole = to_members(done_b, width, entries, "analysis_b")
    whole = pairs_to_members(place, done_a, 0, whole, "analysis_a")
    return whole[:, None]


def solution(mesh):
    in_specs = (
        P("mem", "reg", None, None),
        P("mem", "reg", None, None),
        P("reg", None, None),
        P("reg", None, None),
        P("reg", "mem"),
        P("reg", "mem", None),
    )
    out_specs = P("mem", "reg", None, None)
    return jax.shard_map(body, mesh=mesh, in_specs=in_specs, out_specs=out_specs, check_vma=False)
```

```python
import functools

import jax
import jax.numpy as jnp
from jax import lax
from jax.experimental import pallas as pl
from jax.experimental.pallas import tpu as pltpu
from jax.sharding import PartitionSpec as P

INNOV_ROWS = 16
SLOT_CHUNK = 256
MEMBER_TILE = 16
TRANSFORM_CHUNK = 256
TILE_A = 128
TILE_B = 512
MIB = 1024 * 1024


def fetch_tiles(source_ref, start, stage, arrived, use):
    width = stage.shape[2]
    tiles = []
    for number in range(stage.shape[0] // MEMBER_TILE):
        rows = pl.ds(number * MEMBER_TILE, MEMBER_TILE)
        copy = pltpu.make_async_copy(
            source_ref.at[rows, :, pl.ds(start, width)], stage.at[rows], arrived.at[number]
        )
        copy.start()
        tiles.append((copy, rows))
    for copy, rows in tiles:
        copy.wait()
        use(rows)


def to_blocks_kernel(start, state_ref, out_ref, stage, turned, arrived, sent):
    stores = []

    def use(rows):
        turned[:, rows, :] = jnp.swapaxes(stage[rows], 0, 1)
        store = pltpu.make_async_copy(
            turned.at[:, rows, :], out_ref.at[:, rows, :], sent.at[len(stores)]
        )
        store.start()
        stores.append(store)

    fetch_tiles(state_ref, start, stage, arrived, use)
    for store in stores:
        store.wait()


def to_blocks(state, start, width, name):
    members, blocks, _ = state.shape
    hbm = pl.BlockSpec(memory_space=pltpu.HBM)
    return pl.pallas_call(
        functools.partial(to_blocks_kernel, start),
        in_specs=[hbm],
        out_specs=hbm,
        out_shape=jax.ShapeDtypeStruct((blocks, members, width), state.dtype),
        scratch_shapes=[
            pltpu.VMEM((members, blocks, width), state.dtype),
            pltpu.VMEM((blocks, members, width), state.dtype),
            pltpu.SemaphoreType.DMA((members // MEMBER_TILE,)),
            pltpu.SemaphoreType.DMA((members // MEMBER_TILE,)),
        ],
        compiler_params=pltpu.CompilerParams(vmem_limit_bytes=60 * MIB),
        cost_estimate=pl.CostEstimate(
            flops=0, bytes_accessed=4 * members * blocks * width, transcendentals=0
        ),
        name=name,
    )(state)


def pool_kernel(obs_ref, innov_ref, out_ref, stage, arrived):
    members = obs_ref.shape[0]

    def use(rows):
        out_ref[:, rows, :] = jnp.swapaxes(stage[rows], 0, 1)

    shape = (out_ref.shape[0], INNOV_ROWS, out_ref.shape[2])
    out_ref[:, members:, :] = jnp.broadcast_to(innov_ref[...][:, None, :], shape)
    fetch_tiles(obs_ref, 0, stage, arrived, use)


def pool_rows(obs, innov):
    members, blocks, depth = obs.shape
    rows = members + INNOV_ROWS
    vmem = pl.BlockSpec(memory_space=pltpu.VMEM)
    return pl.pallas_call(
        pool_kernel,
        in_specs=[pl.BlockSpec(memory_space=pltpu.HBM), vmem],
        out_specs=vmem,
        out_shape=jax.ShapeDtypeStruct((blocks, rows, depth), obs.dtype),
        scratch_shapes=[
            pltpu.VMEM((members, blocks, depth), obs.dtype),
            pltpu.SemaphoreType.DMA((members // MEMBER_TILE,)),
        ],
        compiler_params=pltpu.CompilerParams(vmem_limit_bytes=60 * MIB),
        cost_estimate=pl.CostEstimate(
            flops=0, bytes_accessed=4 * rows * blocks * depth, transcendentals=0
        ),
        name="pool_rows",
    )(obs, innov)


def gather_kernel(place_ref, own_ref, up_ref, down_ref, idx_ref, out_ref, inn_ref, stacked):
    block = pl.program_id(0) ^ place_ref[0]
    blocks, rows, depth = own_ref.shape
    members = out_ref.shape[1]
    slots = out_ref.shape[2]
    west = jnp.maximum(block - 1, 0)
    east = jnp.minimum(block + 1, blocks - 1)
    sources = (
        own_ref[block, :rows],
        up_ref[block, :rows],
        down_ref[block, :rows],
        jnp.where(block > 0, own_ref[west, :rows], 0.0),
        jnp.where(block < blocks - 1, own_ref[east, :rows], 0.0),
    )
    for number, source in enumerate(sources):
        stacked[number * rows : (number + 1) * rows] = source.astype(jnp.bfloat16)
    columns = lax.broadcasted_iota(jnp.int32, (depth, SLOT_CHUNK), 0)

    @pl.loop(0, slots // SLOT_CHUNK)
    def _(chunk):
        where = pl.ds(pl.multiple_of(chunk * SLOT_CHUNK, SLOT_CHUNK), SLOT_CHUNK)
        picks = idx_ref[pl.ds(block, 1), where]
        source = sum((picks >= number * depth).astype(jnp.int32) for number in range(1, 5))
        one_hot = jnp.where(columns == picks - source * depth, 1.0, 0.0).astype(jnp.bfloat16)
        products = jnp.dot(stacked[...], one_hot, preferred_element_type=jnp.float32)
        chosen = products[:rows]
        for number in range(1, 5):
            part = products[number * rows : (number + 1) * rows]
            chosen = jnp.where(source == number, part, chosen)
        out_ref[0, :, where] = chosen[:members].astype(jnp.bfloat16)

        @pl.when(pl.program_id(0) == 0)
        def _():
            inn_ref[:, where] = chosen[members:].astype(jnp.bfloat16)


def gather_chosen(place, own, up, down, picks):
    blocks, rows, depth = own.shape
    members = rows - INNOV_ROWS
    slots = picks.shape[1]
    vmem = pl.BlockSpec(memory_space=pltpu.VMEM)
    return pl.pallas_call(
        gather_kernel,
        grid=(blocks,),
        in_specs=[pl.BlockSpec(memory_space=pltpu.SMEM)] + [vmem] * 4,
        out_specs=[
            pl.BlockSpec((1, members, slots), lambda k: (k, 0, 0)),
            pl.BlockSpec((INNOV_ROWS, slots), lambda k: (0, 0)),
        ],
        out_shape=[
            jax.ShapeDtypeStruct((blocks, members, slots), jnp.bfloat16),
            jax.ShapeDtypeStruct((INNOV_ROWS, slots), jnp.bfloat16),
        ],
        scratch_shapes=[pltpu.VMEM((5 * rows, depth), jnp.bfloat16)],
        compiler_params=pltpu.CompilerParams(vmem_limit_bytes=40 * MIB),
        cost_estimate=pl.CostEstimate(flops=0, bytes_accessed=rows * slots, transcendentals=0),
        name="gather_chosen",
    )(place, own, up, down, picks)


def store_tiles(out_ref, start, stage, sent, make):
    width = stage.shape[2]
    copies = []
    for number in range(stage.shape[0] // MEMBER_TILE):
        rows = pl.ds(number * MEMBER_TILE, MEMBER_TILE)
        stage[rows] = make(rows)
        copy = pltpu.make_async_copy(
            stage.at[rows], out_ref.at[rows, :, pl.ds(start, width)], sent.at[number]
        )
        copy.start()
        copies.append(copy)
    for copy in copies:
        copy.wait()


def to_members_kernel(start, part_ref, out_ref, stage, sent):
    store_tiles(out_ref, start, stage, sent, lambda rows: jnp.swapaxes(part_ref[:, rows, :], 0, 1))


def pairs_to_members_kernel(start, place_ref, whole_ref, *refs):
    *part_refs, out_ref, turned, stage, sent = refs
    del whole_ref

    def make(rows):
        for number, ref in enumerate(part_refs):
            turned[place_ref[0] ^ number] = ref[rows]
        return jnp.swapaxes(turned[...], 0, 1)

    store_tiles(out_ref, start, stage, sent, make)


def to_members(part, start, entries, name):
    blocks, members, width = part.shape
    return pl.pallas_call(
        functools.partial(to_members_kernel, start),
        in_specs=[pl.BlockSpec(memory_space=pltpu.VMEM)],
        out_specs=pl.BlockSpec(memory_space=pltpu.HBM),
        out_shape=jax.ShapeDtypeStruct((members, blocks, entries), part.dtype),
        scratch_shapes=[
            pltpu.VMEM((members, blocks, width), part.dtype),
            pltpu.SemaphoreType.DMA((members // MEMBER_TILE,)),
        ],
        compiler_params=pltpu.CompilerParams(vmem_limit_bytes=16 * MIB),
        cost_estimate=pl.CostEstimate(
            flops=0, bytes_accessed=4 * members * blocks * width, transcendentals=0
        ),
        name=name,
    )(part)


def pairs_to_members(place, parts, start, whole, name):
    blocks = len(parts)
    members, width = parts[0].shape
    hbm = pl.BlockSpec(memory_space=pltpu.HBM)
    return pl.pallas_call(
        functools.partial(pairs_to_members_kernel, start),
        in_specs=[pl.BlockSpec(memory_space=pltpu.SMEM), hbm]
        + [pl.BlockSpec(memory_space=pltpu.VMEM)] * blocks,
        out_specs=hbm,
        out_shape=jax.ShapeDtypeStruct(whole.shape, whole.dtype),
        scratch_shapes=[
            pltpu.VMEM((blocks, MEMBER_TILE, width), whole.dtype),
            pltpu.VMEM((members, blocks, width), whole.dtype),
            pltpu.SemaphoreType.DMA((members // MEMBER_TILE,)),
        ],
        input_output_aliases={1: 0},
        compiler_params=pltpu.CompilerParams(vmem_limit_bytes=16 * MIB),
        cost_estimate=pl.CostEstimate(
            flops=0, bytes_accessed=4 * members * blocks * width, transcendentals=0
        ),
        name=name,
    )(place, whole, *parts)


def transform_kernel(place_ref, tally_ref, weight_ref, innov_ref, *refs):
    *part_refs, out_ref, obs_ref = refs[:-8]
    weighted, precision, root, step, root_next, step_next, inverse, arrived = refs[-8:]
    count_k, slots = obs_ref.shape
    members = count_k // len(part_refs)
    copies = []
    for number, ref in enumerate(part_refs):
        at = pl.multiple_of((place_ref[0] ^ number) * members, members)
        copies.append(
            pltpu.make_async_copy(ref, obs_ref.at[pl.ds(at, members)], arrived.at[number])
        )
    for copy in copies:
        copy.start()
    for copy in copies:
        copy.wait()
    spare = count_k - 1.0
    chunks = count_k // TRANSFORM_CHUNK
    live = lax.broadcasted_iota(jnp.int32, (1, slots), 1) < tally_ref[0, 0]
    obs_weight = jnp.where(live, weight_ref[...], 0.0)

    def span(chunk):
        return pl.ds(pl.multiple_of(chunk * TRANSFORM_CHUNK, TRANSFORM_CHUNK), TRANSFORM_CHUNK)

    def on_diagonal(chunk, value):
        rows = lax.broadcasted_iota(jnp.int32, (count_k, TRANSFORM_CHUNK), 0)
        columns = lax.broadcasted_iota(jnp.int32, (count_k, TRANSFORM_CHUNK), 1)
        return jnp.where(rows == columns + chunk * TRANSFORM_CHUNK, value, 0.0)

    def matmul(left, right):
        return jnp.dot(left, right, preferred_element_type=jnp.float32)

    def by_rows(left, right):
        return lax.dot_general(
            left, right, (((1,), (1,)), ((), ())), preferred_element_type=jnp.float32
        )

    def precise(row, matrix):
        high = row.astype(jnp.bfloat16)
        rest = row - high.astype(jnp.float32)
        middle = rest.astype(jnp.bfloat16)
        low = (rest - middle.astype(jnp.float32)).astype(jnp.bfloat16)
        return (matmul(low, matrix) + matmul(middle, matrix)) + matmul(high, matrix)

    def weigh(chunk, trace):
        at = span(chunk)
        scaled = (obs_ref[at, :].astype(jnp.float32) * obs_weight).astype(jnp.bfloat16)
        weighted[at, :] = scaled
        product = by_rows(obs_ref[...], scaled)
        precision[:, at] = product
        return trace + jnp.sum(on_diagonal(chunk, product))

    trace = lax.fori_loop(0, chunks, weigh, jnp.float32(0.0))
    trace_mean = trace / count_k + spare
    scale = 1.0 / trace_mean
    gain = by_rows(innov_ref[...], weighted[...])

    @pl.loop(0, chunks)
    def _(chunk):
        at = span(chunk)
        first = ((precision[:, at] + on_diagonal(chunk, spare)) * scale).astype(jnp.bfloat16)
        root[:, at] = first
        step[:, at] = (on_diagonal(chunk, 1.5) - 0.5 * first.astype(jnp.float32)).astype(jnp.bfloat16)

    @pl.loop(0, chunks)
    def _(chunk):
        at = span(chunk)
        root_next[:, at] = matmul(step[...], root[:, at]).astype(jnp.bfloat16)

    @pl.loop(0, chunks)
    def _(chunk):
        at = span(chunk)
        product = matmul(root_next[...], step[:, at])
        step_next[:, at] = (on_diagonal(chunk, 1.5) - 0.5 * product).astype(jnp.bfloat16)

    @pl.loop(0, chunks)
    def _(chunk):
        at = span(chunk)
        inverse[:, at] = matmul(step[...], step_next[:, at]).astype(jnp.bfloat16)

    inner = precise(gain, inverse[...])
    mean_weight = precise(inner, inverse[...])[:1] * scale
    spread_factor = jnp.sqrt(jnp.full((1, slots), spare * scale, jnp.float32))
    out_ref[...] = (
        spread_factor[:, :count_k] * inverse[...].astype(jnp.float32) + mean_weight
    ).astype(jnp.bfloat16)


def ensemble_transform(place, tally, weight, innov, parts):
    members, slots = parts[0].shape
    count_k = members * len(parts)
    vmem = pl.BlockSpec(memory_space=pltpu.VMEM)
    square = pltpu.VMEM((count_k, count_k), jnp.bfloat16)
    return pl.pallas_call(
        transform_kernel,
        in_specs=[pl.BlockSpec(memory_space=pltpu.SMEM)] * 2
        + [vmem] * 2
        + [pl.BlockSpec(memory_space=pl.ANY)] * len(parts),
        out_specs=vmem,
        out_shape=jax.ShapeDtypeStruct((count_k, count_k), jnp.bfloat16),
        scratch_shapes=[
            pltpu.VMEM((count_k, slots), jnp.bfloat16),
            pltpu.VMEM((count_k, slots), jnp.bfloat16),
            pltpu.VMEM((count_k, count_k), jnp.float32),
            square, square, square, square, square,
            pltpu.SemaphoreType.DMA((len(parts),)),
        ],
        compiler_params=pltpu.CompilerParams(vmem_limit_bytes=40 * MIB),
        cost_estimate=pl.CostEstimate(
            flops=0,
            bytes_accessed=count_k * slots,
            transcendentals=0,
        ),
        name="transform",
    )(place, tally, weight, innov, *parts)


def analysis_kernel(in_pairs, place_ref, transform_ref, state_ref, out_ref, stage):
    blocks, members, width = out_ref.shape
    state = state_ref[...].astype(jnp.float32)
    state_mean = jnp.sum(state, axis=0, keepdims=True) * (1.0 / state.shape[0])
    perturb = (state - state_mean).astype(jnp.bfloat16)
    increment = jnp.dot(transform_ref[...], perturb, preferred_element_type=jnp.float32)
    result = (state_mean + increment).astype(jnp.bfloat16).reshape(out_ref.shape)
    if in_pairs:
        stage[...] = result
        for number in range(blocks):
            out_ref[number] = stage[place_ref[0] ^ number]
    else:
        out_ref[...] = result


def analysed(place, transform, part, in_pairs, tile, name):
    blocks, members, width = part.shape
    count_k = blocks * members
    return pl.pallas_call(
        functools.partial(analysis_kernel, in_pairs),
        grid=(width // tile,),
        in_specs=[
            pl.BlockSpec(memory_space=pltpu.SMEM),
            pl.BlockSpec(memory_space=pltpu.VMEM),
            pl.BlockSpec((count_k, tile), lambda i: (0, i)),
        ],
        out_specs=pl.BlockSpec((blocks, members, tile), lambda i: (0, 0, i)),
        out_shape=jax.ShapeDtypeStruct(part.shape, jnp.bfloat16),
        scratch_shapes=[pltpu.VMEM((blocks, members, tile), jnp.bfloat16)],
        compiler_params=pltpu.CompilerParams(vmem_limit_bytes=32 * MIB),
        cost_estimate=pl.CostEstimate(
            flops=0,
            bytes_accessed=count_k * width,
            transcendentals=0,
        ),
        name=name,
    )(place, transform, part.reshape(count_k, width))


def body(
    prior_members_field,
    measure_space_deviations,
    measured_minus_predicted,
    measure_pool_indices,
    active_measure_tally,
    tapered_error_weight,
):
    place = lax.axis_index("mem").astype(jnp.int32).reshape(1)
    strips = lax.axis_size("reg")
    devices = lax.axis_size("mem")
    entries = prior_members_field.shape[3]
    to_next = [(i, i + 1) for i in range(strips - 1)]
    to_last = [(i + 1, i) for i in range(strips - 1)]

    def exchange(x):
        return lax.all_to_all(x, "mem", split_axis=0, concat_axis=0, tiled=True)

    def swap(x, number):
        return lax.ppermute(x, "mem", [(i, i ^ number) for i in range(devices)])

    half = devices // 2
    width = entries // 2
    state = prior_members_field[:, 0]
    state_a = to_blocks(state, 0, width, "state_a")
    devs, state_a = lax.optimization_barrier((measure_space_deviations[:, 0], state_a))
    state_a = exchange(state_a)
    pool = pool_rows(devs, measured_minus_predicted[0])
    up = lax.ppermute(pool, "reg", to_next)
    down = lax.ppermute(pool, "reg", to_last)
    chosen, innov = gather_chosen(place, pool, up, down, measure_pool_indices[0])
    far = [swap(chosen[k], k) for k in range(half, devices)]
    near = [chosen[0]] + [swap(chosen[k], k) for k in range(1, half)]
    state_b = to_blocks(state, width, entries - width, "state_b")
    near, far, state_a, state_b = lax.optimization_barrier((near, far, state_a, state_b))
    state_b = exchange(state_b)
    transform = ensemble_transform(
        place, active_measure_tally, tapered_error_weight[0], innov, near + far
    )
    done_a = analysed(place, transform, state_a, True, TILE_A, "analysed_a")
    transform, done_a = lax.optimization_barrier((transform, done_a))
    done_a = [done_a[0]] + [swap(done_a[k], k) for k in range(1, devices)]
    done_b = analysed(place, transform, state_b, False, TILE_B, "analysed_b")
    done_b, *done_a[half : half + 2] = lax.optimization_barrier(
        (done_b, *done_a[half : half + 2])
    )
    done_b = exchange(done_b)
    whole = to_members(done_b, width, entries, "analysis_b")
    whole = pairs_to_members(place, done_a, 0, whole, "analysis_a")
    return whole[:, None]


def solution(mesh):
    in_specs = (
        P("mem", "reg", None, None),
        P("mem", "reg", None, None),
        P("reg", None, None),
        P("reg", None, None),
        P("reg", "mem"),
        P("reg", "mem", None),
    )
    out_specs = P("mem", "reg", None, None)
    return jax.shard_map(body, mesh=mesh, in_specs=in_specs, out_specs=out_specs, check_vma=False)
```
